128 devices in a mesh: table: 16 (over z, x), seq: 2 (over core), dp: 4 (over y).
Axes of the slice: x: 4, y: 4, z: 4, core: 2. Of those that a mesh axis runs over, the one named last changes fastest.
Arguments:
- table_wide: bfloat16 [256, 262144], P(None, ('table', 'seq', 'dp')), may hold values from -6 to 6
- table_mid: bfloat16 [128, 262144], P(None, ('table', 'seq', 'dp')), may hold values from -6 to 6
- table_narrow: bfloat16 [64, 262144], P(None, ('table', 'seq', 'dp')), may hold values from -6 to 6
- table_thin: bfloat16 [32, 262144], P(None, ('table', 'seq', 'dp')), may hold values from -6 to 6
- band_proj: bfloat16 [480, 512], replicated, may hold values from -0.5 to 0.5
- first_conv_weight: bfloat16 [1536, 512], replicated, may hold values from -0.15625 to 0.15625
- first_conv_bias: float32 [512], replicated, may hold values from -3 to 3
- gain_first: float32 [512], replicated, may hold values from 0.25 to 1.75
- offset_first: float32 [512], replicated, may hold values from -3 to 3
- second_conv_weight: bfloat16 [1536, 512], replicated, may hold values from -0.15625 to 0.15625
- second_conv_bias: float32 [512], replicated, may hold values from -3 to 3
- gain_second: float32 [512], replicated, may hold values from 0.25 to 1.75
- offset_second: float32 [512], replicated, may hold values from -3 to 3
- slot_event: int32 [64, 2, 128, 8], P(('table', 'dp'), 'seq'), may hold values from 0 to 511, as said below
- slot_counts: int32 [64, 2, 128], P(('table', 'dp'), 'seq'), may hold values from 0 to 8, as said below
- slot_band: int32 [64, 2, 128, 8], P(('table', 'dp'), 'seq'), may hold values from 0 to 3
- slot_row: int32 [64, 2, 128, 8], P(('table', 'dp'), 'seq'), may hold values from 0 to 2047
- out_grad: bfloat16 [64, 1024, 512], P(('table', 'dp'), 'seq'), may hold values from -6 to 6
Outputs:
- block_out: bfloat16 [64, 1024, 512], P(('table', 'dp'), 'seq')
- grad_table_wide: bfloat16 [256, 262144], P(None, ('table', 'seq', 'dp'))
- grad_table_mid: bfloat16 [128, 262144], P(None, ('table', 'seq', 'dp'))
- grad_table_narrow: bfloat16 [64, 262144], P(None, ('table', 'seq', 'dp'))
- grad_table_thin: bfloat16 [32, 262144], P(None, ('table', 'seq', 'dp'))
- grad_proj: float32 [480, 512], replicated
- grad_conv_first: float32 [1536, 512], replicated
- grad_conv_second: float32 [1536, 512], replicated
- grad_vectors: float32 [6, 512], replicated
The draws below stay inside these ranges and needn't reach their ends.
Inputs may be any that keep to these rules, and one draw needn't show every extreme that they name: `slot_counts`: counts of one device's block sum to 512; one owner, the same for every device, has exactly 8 live slots from every device. `slot_event`: live slots are the first slot_counts slots toward each owner; the live slots of one device's block name each of its 512 positions exactly once; other slots hold arbitrary positions.
All inputs are finite; a program needn't handle non-finite values.
Results may differ from the reference program's by a relative error of at most 0.0085.
Values may be sent and summed in bfloat16 or wider, within the bound.
A program may use at most 128 MiB of HBM per device.

```python
import math
import jax
import jax.numpy as jnp
from jax import lax

CH = 512
W0 = 256
W1 = 128
W2 = 64
W3 = 32
DILATION_STEP = 4
LEN_DEV = 512
ROWS_DEV = 2048
BANDW = 480
CAP = 8
HISTS = 64
LENGTH = 1024
EVENTS = 65536
ROWS = 262144
N_SEQ = 2
DEVICES = 128


def slot_layout(key):
    blocks_count = HISTS * N_SEQ
    rest_count = LEN_DEV - CAP
    cell_total = (DEVICES - 1) * CAP
    hot_key, block_key = jax.random.split(key)
    hottest = jax.random.randint(hot_key, (), 0, DEVICES, dtype=jnp.int32)

    def one_block(block_seed):
        perm_key, cell_key, dead_key = jax.random.split(block_seed, 3)
        event_order = jax.random.permutation(perm_key, LEN_DEV).astype(jnp.int32)
        chosen = jnp.sort(jax.random.permutation(cell_key, cell_total)[:rest_count].astype(jnp.int32))
        others = chosen // CAP
        owner_ids = others + (others >= hottest).astype(jnp.int32)
        owner_range = jnp.arange(DEVICES, dtype=jnp.int32)
        matches = (owner_ids[:, None] == owner_range[None, :]).astype(jnp.int32)
        other_counts = jnp.sum(matches, axis=0)
        starts = jnp.cumsum(other_counts) - other_counts
        slot_rank = jnp.arange(rest_count, dtype=jnp.int32) - starts[owner_ids]
        counts = other_counts + CAP * (owner_range == hottest).astype(jnp.int32)
        events = jax.random.randint(dead_key, (DEVICES, CAP), 0, LEN_DEV, dtype=jnp.int32)
        events = events.at[hottest].set(event_order[:CAP])
        events = events.at[owner_ids, slot_rank].set(event_order[CAP:])
        return (events, counts)
    events, counts = jax.vmap(one_block)(jax.random.split(block_key, blocks_count))
    return (events.reshape(HISTS, N_SEQ, DEVICES, CAP), counts.reshape(HISTS, N_SEQ, DEVICES))


def draw_slot_event(key, part):
    return slot_layout(key)[0]


def draw_slot_counts(key, part):
    return slot_layout(key)[1]


def set_ends(values, own_key, low, largest):
    longest = values.shape.index(max(values.shape))
    spots = []
    for shift in (0, 1):
        where = [jax.random.randint(jax.random.fold_in(own_key, axis), (), 0, length) for axis, length in enumerate(values.shape)]
        where[longest] = (where[longest] + shift) % values.shape[longest]
        spots.append(tuple(where))
    return values.at[spots[0]].set(low).at[spots[1]].set(largest)


def block_levels(own_key, shape, cuts, low, high):
    def one(dim, blocks):
        heights = jax.random.uniform(jax.random.fold_in(jax.random.fold_in(own_key, 6), dim), (blocks,), jnp.float32, low / len(cuts), high / len(cuts))
        return jnp.repeat(jnp.exp(heights), shape[dim] // blocks).reshape((-1,) + (1,) * (len(shape) - dim - 1))

    loudness = one(*cuts[0])
    for cut in cuts[1:]:
        loudness = loudness * one(*cut)
    return loudness


def gaussian(stream_key, extent, deviation, reach, pieces=(), kind=jnp.bfloat16):
    loudness = block_levels(stream_key, extent, pieces, -0.22, 0.18) if pieces else 1.0
    values = jax.random.normal(stream_key, extent, jnp.float32) * deviation * loudness
    return jnp.minimum(jnp.maximum(values, -reach), reach).astype(kind)


def setup_inputs(seed: int = 0) -> dict:
    keys = jax.random.split(jax.random.key(seed), 19)
    return {
        "table_wide": gaussian(keys[0], (W0, ROWS), 1.0, 6.0, ((1, 128),)),
        "table_mid": gaussian(keys[1], (W1, ROWS), 1.0, 6.0, ((1, 128),)),
        "table_narrow": gaussian(keys[2], (W2, ROWS), 1.0, 6.0, ((1, 128),)),
        "table_thin": gaussian(keys[3], (W3, ROWS), 1.0, 6.0, ((1, 128),)),
        "band_proj": gaussian(keys[4], (BANDW, CH), W1 ** -0.5, 0.5),
        "first_conv_weight": gaussian(keys[5], (3 * CH, CH), (3 * CH) ** -0.5, 0.15625),
        "first_conv_bias": gaussian(keys[6], (CH,), 0.5, 3.0, (), jnp.float32),
        "gain_first": jnp.clip(1.0 + 0.15 * jax.random.normal(keys[7], (CH,), jnp.float32), 0.25, 1.75),
        "offset_first": gaussian(keys[8], (CH,), 0.5, 3.0, (), jnp.float32),
        "second_conv_weight": gaussian(keys[9], (3 * CH, CH), (3 * CH) ** -0.5, 0.15625),
        "second_conv_bias": gaussian(keys[10], (CH,), 0.5, 3.0, (), jnp.float32),
        "gain_second": jnp.clip(1.0 + 0.15 * jax.random.normal(keys[11], (CH,), jnp.float32), 0.25, 1.75),
        "offset_second": gaussian(keys[12], (CH,), 0.5, 3.0, (), jnp.float32),
        "slot_event": draw_slot_event(jax.random.fold_in(keys[18], 71), 0),
        "slot_counts": draw_slot_counts(jax.random.fold_in(keys[18], 71), 0),
        "slot_band": set_ends(jax.random.randint(keys[15], (HISTS, N_SEQ, DEVICES, CAP), 0, 4), jax.random.fold_in(keys[15], 1), 0, 3).astype(jnp.int32),
        "slot_row": set_ends(jax.random.randint(keys[16], (HISTS, N_SEQ, DEVICES, CAP), 0, ROWS_DEV), jax.random.fold_in(keys[16], 1), 0, ROWS_DEV - 1).astype(jnp.int32),
        "out_grad": gaussian(keys[17], (HISTS, LENGTH, CH), 1.0, 6.0, ((0, 64), (1, 2))),
    }


layer_eps = 1e-05

def fetch_rows(tables, row_ids, band_ids):
    widest = tables[0].shape[0]
    gathered = jnp.zeros((row_ids.shape[0], widest), tables[0].dtype)
    for band_index, band_table in enumerate(tables):
        columns = jnp.take(band_table, row_ids, axis=1).T
        padded = jnp.pad(columns, ((0, 0), (0, widest - band_table.shape[0])))
        gathered = jnp.where((band_ids == band_index)[:, None], padded, gathered)
    return gathered

def project_rows(gathered, band_ids, band_proj, widths):
    result = jnp.zeros((gathered.shape[0], band_proj.shape[1]), jnp.float32)
    offset = 0
    for band_index, band_width in enumerate(widths):
        partial_value = jnp.dot(gathered[:, :band_width], band_proj[offset:offset + band_width], preferred_element_type=jnp.float32)
        result = jnp.where((band_ids == band_index)[:, None], partial_value, result)
        offset += band_width
    return result.astype(jnp.bfloat16)

def projection_grad(gathered, band_ids, grad_rows, widths):
    blocks = []
    for band_index, band_width in enumerate(widths):
        picked = jnp.where((band_ids == band_index)[:, None], gathered[:, :band_width], jnp.zeros_like(gathered[:, :band_width]))
        blocks.append(lax.dot_general(picked, grad_rows, (((0,), (0,)), ((), ())), preferred_element_type=jnp.float32))
    return jnp.concatenate(blocks, axis=0)

def row_grads(grad_rows, band_ids, band_proj, widths):
    widest = widths[0]
    result = jnp.zeros((grad_rows.shape[0], widest), jnp.float32)
    offset = 0
    for band_index, band_width in enumerate(widths):
        partial_value = lax.dot_general(grad_rows, band_proj[offset:offset + band_width], (((1,), (1,)), ((), ())), preferred_element_type=jnp.float32)
        partial_value = jnp.pad(partial_value, ((0, 0), (0, widest - band_width)))
        result = jnp.where((band_ids == band_index)[:, None], partial_value, result)
        offset += band_width
    return lax.optimization_barrier(result.astype(jnp.bfloat16))

def scatter_rows(row_grad, row_ids, band_ids, widths, row_count):
    widened = row_grad.astype(jnp.float32)
    outputs = []
    for band_index, band_width in enumerate(widths):
        picked = jnp.where((band_ids == band_index)[:, None], widened[:, :band_width], jnp.zeros_like(widened[:, :band_width]))
        summed = jnp.zeros((band_width, row_count), jnp.float32).at[:, row_ids].add(picked.T)
        outputs.append(summed.astype(jnp.bfloat16))
    return tuple(outputs)

def stack_past(extended, dilation_factor):
    length_out = extended.shape[0] - 2 * dilation_factor
    tap_rows = [extended[(2 - tap_index) * dilation_factor:(2 - tap_index) * dilation_factor + length_out] for tap_index in range(3)]
    return jnp.concatenate(tap_rows, axis=1)

def stack_future(extended, dilation_factor):
    length_out = extended.shape[0] - 2 * dilation_factor
    tap_rows = [extended[tap_index * dilation_factor:tap_index * dilation_factor + length_out] for tap_index in range(3)]
    return jnp.concatenate(tap_rows, axis=1)

def convolution_forward(extended, weight, bias_vec, dilation_factor):
    return jnp.dot(stack_past(extended, dilation_factor), weight, preferred_element_type=jnp.float32) + bias_vec

def convolution_input_gradient(extended, weight, dilation_factor):
    tap_rows = stack_future(extended, dilation_factor)
    channel_count = weight.shape[1]
    tap_rows = tap_rows.reshape(tap_rows.shape[0], 3, channel_count)
    kernel = weight.reshape(3, weight.shape[0] // 3, channel_count)
    return lax.dot_general(tap_rows, kernel, (((1, 2), (0, 2)), ((), ())), preferred_element_type=jnp.float32)

def convolution_weight_gradient(extended, grad_rows, dilation_factor):
    return lax.dot_general(stack_past(extended, dilation_factor), grad_rows, (((0,), (0,)), ((), ())), preferred_element_type=jnp.float32)

def norm_act(hidden, norm_gain, offset):
    centre = hidden - lax.optimization_barrier(jnp.mean(hidden, axis=-1, keepdims=True))
    spread = lax.optimization_barrier(jnp.mean(centre * centre, axis=-1, keepdims=True))
    return jax.nn.gelu(centre * lax.rsqrt(spread + layer_eps) * norm_gain + offset, approximate=True)

def norm_back(hidden, norm_gain, offset, cotangent):
    primal_out, pullback = jax.vjp(norm_act, hidden, norm_gain, offset)
    return pullback(cotangent)

def history_pass(embedded_items, out_grad, weights):
    first_conv_weight, first_conv_bias, gain_first, offset_first, second_conv_weight, second_conv_bias, gain_second, offset_second = weights
    channel_count = embedded_items.shape[1]
    first_padding = jnp.zeros((2 * DILATION_STEP, channel_count), embedded_items.dtype)
    second_padding = jnp.zeros((4 * DILATION_STEP, channel_count), embedded_items.dtype)
    extended_embedding = jnp.concatenate([first_padding, embedded_items])
    first_hidden_state = convolution_forward(extended_embedding, first_conv_weight, first_conv_bias, DILATION_STEP)
    act_first = norm_act(first_hidden_state, gain_first, offset_first).astype(jnp.bfloat16)
    extended_activation = jnp.concatenate([second_padding, act_first])
    second_hidden_state = convolution_forward(extended_activation, second_conv_weight, second_conv_bias, 2 * DILATION_STEP)
    act_second = norm_act(second_hidden_state, gain_second, offset_second)
    block_out = (embedded_items.astype(jnp.float32) + act_second).astype(jnp.bfloat16)
    incoming_gradient = out_grad.astype(jnp.float32)
    second_gradient, gain_two, offset_two = norm_back(second_hidden_state, gain_second, offset_second, incoming_gradient)
    second_gradient = lax.optimization_barrier(second_gradient.astype(jnp.bfloat16))
    activation_gradient = convolution_input_gradient(jnp.concatenate([second_gradient, second_padding]), second_conv_weight, 2 * DILATION_STEP)
    first_gradient, gain_one, offset_one = norm_back(first_hidden_state, gain_first, offset_first, activation_gradient)
    first_gradient = lax.optimization_barrier(first_gradient.astype(jnp.bfloat16))
    embedding_gradient = (incoming_gradient + convolution_input_gradient(jnp.concatenate([first_gradient, first_padding]), first_conv_weight, DILATION_STEP)).astype(jnp.bfloat16)
    first_convolution = convolution_weight_gradient(extended_embedding, first_gradient, DILATION_STEP)
    second_convolution = convolution_weight_gradient(extended_activation, second_gradient, 2 * DILATION_STEP)
    bias_one = lax.optimization_barrier(jnp.sum(first_gradient.astype(jnp.float32), axis=0))
    bias_two = lax.optimization_barrier(jnp.sum(second_gradient.astype(jnp.float32), axis=0))
    return (block_out, embedding_gradient, (first_convolution, second_convolution, bias_one, gain_one, offset_one, bias_two, gain_two, offset_two))

def reference(table_wide, table_mid, table_narrow, table_thin, band_proj, first_conv_weight, first_conv_bias, gain_first, offset_first, second_conv_weight, second_conv_bias, gain_second, offset_second, slot_event, slot_counts, slot_band, slot_row, out_grad):
    tables = (table_wide, table_mid, table_narrow, table_thin)
    widths = tuple((band_table.shape[0] for band_table in tables))
    blocks_count = HISTS * N_SEQ
    owners = slot_counts.shape[2]
    live_mask = jnp.arange(CAP, dtype=jnp.int32)[None, None, None, :] < slot_counts[..., None]
    global_row = slot_row + (jnp.arange(owners, dtype=jnp.int32) * ROWS_DEV)[None, None, :, None]
    target = jnp.where(live_mask, slot_event, LEN_DEV).reshape(blocks_count, owners * CAP)

    def place_values(values):
        flat_values = values.reshape(blocks_count, owners * CAP)

        def place_one(target_row, value_row):
            return jnp.zeros((LEN_DEV,), jnp.int32).at[target_row].set(value_row, mode='drop')
        return jax.vmap(place_one)(target, flat_values).reshape(HISTS * LENGTH)
    event_row = place_values(global_row)
    event_band = place_values(slot_band)
    gathered = fetch_rows(tables, event_row, event_band)
    embedded_items = project_rows(gathered, event_band, band_proj, widths).reshape(HISTS, LENGTH, CH)
    weights = (first_conv_weight, first_conv_bias, gain_first, offset_first, second_conv_weight, second_conv_bias, gain_second, offset_second)
    zero_grads = (jnp.zeros((3 * CH, CH), jnp.float32), jnp.zeros((3 * CH, CH), jnp.float32)) + tuple((jnp.zeros((CH,), jnp.float32) for unused_index in range(6)))

    def scan_step(running, history_pair):
        block_row, grad_row, grads_now = history_pass(history_pair[0], history_pair[1], weights)
        return (tuple((running_sum + grad_now for running_sum, grad_now in zip(running, grads_now))), (block_row, grad_row))
    running, outputs = lax.scan(scan_step, zero_grads, (embedded_items, out_grad))
    block_out, embedding_gradient = outputs
    grad_scale = 1.0 / math.sqrt(EVENTS)
    flat_grads = embedding_gradient.reshape(HISTS * LENGTH, CH)
    grad_proj = projection_grad(gathered, event_band, flat_grads, widths) * grad_scale
    event_row_grad = row_grads(flat_grads, event_band, band_proj, widths)
    table_out = scatter_rows(event_row_grad, event_row, event_band, widths, ROWS)
    grad_vectors = jnp.stack(running[2:]) * grad_scale
    return (block_out, table_out[0], table_out[1], table_out[2], table_out[3], grad_proj, running[0] * grad_scale, running[1] * grad_scale, grad_vectors)
```

```python
import functools

import jax
import jax.numpy as jnp
from jax import lax
from jax.experimental import pallas as pl
from jax.experimental.pallas import tpu as pltpu
from jax.sharding import PartitionSpec as P

MESH = pl.DeviceIdType.MESH
F32, BF16, I32 = jnp.float32, jnp.bfloat16, jnp.int32
STEP = 4
EPS = 1e-5
NDEV, CAP, SLOTS, LEN, CH, ROWS = 128, 8, 1024, 512, 512, 2048
HALF = 256
BLK = 32
GC = 0.7978845608028654
GA = 0.044715
NT = (((1,), (1,)), ((), ()))
TN = (((0,), (0,)), ((), ()))
BASES = (0, 1536, 3072)
SPANS = (768, 768, 256)
AXES = ("x", "y", "z")


def dot(a, b, dims=None):
    if dims is None:
        return jnp.dot(a, b, preferred_element_type=F32)
    return lax.dot_general(a, b, dims, preferred_element_type=F32)


def gelu_parts(u):
    sq = u * u
    t = jnp.tanh(GC * (u + GA * u * sq))
    half = 0.5 * (1.0 + t)
    slope = half + (0.5 * GC) * u * (1.0 - t * t) * (1.0 + (3.0 * GA) * sq)
    return u * half, slope


def row_mean(v):
    return jnp.sum(v, axis=-1, keepdims=True) * (1.0 / CH)


def fold(v):
    return jnp.sum(v.reshape(v.shape[0] // 8, 8, v.shape[1]), axis=0)


def kernel(
    wide, mid, narrow, thin, proj, w1, w2, og,
    codes, target, sband, b1, g1, o1, b2, g2, o2,
    block_out, t_wide, t_mid, t_narrow, t_thin, grads,
    tcat, pext, w1v, w2v, ogv, relay, fetched, code_sc, onehot, place, msg, answers,
    eband, xm, e32, ehalo_s, ehalo_r, estack, hid, norm1, slope1, rstd1, a32, ahalo_s, ahalo_r, astack,
    bov, g2f, ghalo2_s, ghalo2_r, g1f, ghalo1_s, ghalo1_r, ge, gmsg, gotg, mt, tout,
    own_a, own_b, own_c, xs_a, xs_b, xs_c, xr_a, xr_b, xr_c, u_a, u_b, u_c,
    s1_r, s2_s, s2_r, s3_q, zbuf,
    in_sem, rq_sem, ans_sem, halo_sem, gr_sem, core_sem, ar_sem, fin_sem, out_sem, loc_sem,
):
    t, s, d = lax.axis_index("table"), lax.axis_index("seq"), lax.axis_index("dp")
    sd = s * 4 + d
    me = t * 8 + sd
    coord = {"x": lax.rem(t, 4), "y": d, "z": t // 4}
    other = 1 - s

    def peer(axis, j):
        n = lax.rem(coord[axis] + j, 4)
        if axis == "x":
            return n, (t - coord["x"] + n, s, d)
        if axis == "y":
            return n, (t, s, n)
        return n, (n * 4 + coord["x"], s, d)

    def dev(o):
        return (o // 8, lax.rem(o // 4, 2), lax.rem(o, 4))

    def rcopy(src, dst, send, recv, to):
        return pltpu.make_async_remote_copy(
            src_ref=src, dst_ref=dst, send_sem=send, recv_sem=recv, device_id=to, device_id_type=MESH
        )

    partner = (t, other, d)

    ins = [
        (wide, tcat.at[0:256]), (mid, tcat.at[256:384]), (narrow, tcat.at[384:448]),
        (thin, tcat.at[448:480]), (proj, pext.at[0:480]), (w1, w1v), (w2, w2v), (og, ogv),
    ]
    in_copies = [pltpu.make_async_copy(a, b, in_sem.at[i]) for i, (a, b) in enumerate(ins)]
    for c in in_copies:
        c.start()

    bar = pltpu.get_barrier_semaphore()

    def near(k):
        n = lax.rem(sd + k, 8)
        return n, (t, n // 4, lax.rem(n, 4))

    def far(k):
        n = lax.rem(t + k, 16)
        return n, (n, s, d)

    def sig_near(k, c):
        pl.semaphore_signal(bar, inc=1, device_id=near(k)[1], device_id_type=MESH)
        return c

    def sig_far(k, c):
        pl.semaphore_signal(bar, inc=1, device_id=far(k)[1], device_id_type=MESH)
        return c

    lax.fori_loop(1, 8, sig_near, 0)
    lax.fori_loop(1, 16, sig_far, 0)
    pl.semaphore_wait(bar, 22)

    def ask_near(k, c):
        n, to = near(k)
        rcopy(codes.at[:, n], relay.at[sd], rq_sem.at[0], rq_sem.at[1], to).start()
        return c

    lax.fori_loop(1, 8, ask_near, 0)
    own = pltpu.make_async_copy(codes.at[:, sd], relay.at[sd], loc_sem.at[0])
    own.start()

    hit = lax.broadcasted_iota(I32, (LEN, SLOTS), 0) == target[...]
    place[...] = hit.astype(F32).astype(BF16)
    ev = jnp.sum(jnp.where(hit, sband[...].astype(F32), 0.0), axis=1, keepdims=True)
    eband[...] = jnp.broadcast_to(ev, (LEN, 128))
    pext[480:512] = jnp.zeros((32, CH), BF16)
    tcat[480:512] = jnp.zeros((32, ROWS), BF16)

    own.wait()
    w = rcopy(relay.at[pl.ds(0, 7)], relay.at[pl.ds(0, 7)], rq_sem.at[0], rq_sem.at[1], partner)
    w.wait_recv()

    def ask_far(k, c):
        n, to = far(k)
        rcopy(relay.at[:, n], fetched.at[t], rq_sem.at[2], rq_sem.at[3], to).start()
        return c

    lax.fori_loop(1, 16, ask_far, 0)
    own = pltpu.make_async_copy(relay.at[:, t], fetched.at[t], loc_sem.at[0])
    own.start()
    own.wait()
    w2nd = rcopy(fetched.at[pl.ds(0, 15)], fetched.at[pl.ds(0, 15)], rq_sem.at[2], rq_sem.at[3], partner)
    w2nd.wait_recv()

    got = fetched[...].reshape(NDEV, 1, 128).astype(F32)
    wide_got = jnp.broadcast_to(got, (NDEV, CAP, 128))
    lane = lax.broadcasted_iota(I32, (NDEV, CAP, 128), 2)
    sub = lax.broadcasted_iota(I32, (NDEV, CAP, 128), 1)
    picked = jnp.sum(jnp.where(lane == sub, wide_got, 0.0), axis=-1, keepdims=True)
    code_sc[...] = jnp.broadcast_to(picked, (NDEV, CAP, 128)).reshape(SLOTS, 128).astype(I32)

    for c in in_copies[:4]:
        c.wait()

    lane128 = lax.broadcasted_iota(I32, (HALF, 128), 1)

    def lookup(i, carry):
        cb = lax.rem(me // 32 + i, 4)
        rows = pl.ds(pl.multiple_of(cb * HALF, HALF), HALF)
        code = code_sc[rows]
        row, band = code & (ROWS - 1), code >> 11
        for b in range(ROWS // 128):
            onehot[rows, b * 128 : (b + 1) * 128] = (row == lane128 + b * 128).astype(F32).astype(BF16)
        got_rows = dot(onehot[rows], tcat[...], NT)
        first = jnp.where(
            band == 0, got_rows[:, 0:128], jnp.where(band == 1, got_rows[:, 256:384], got_rows[:, 384:512])
        )
        both = jnp.concatenate(
            [first.reshape(32, 8, 128), got_rows[:, 128:256].reshape(32, 8, 128)], axis=1
        )
        msg[pl.ds(cb * 32, 32)] = both.astype(BF16)

        def send(k, c):
            to = cb * 32 + lax.rem(me + k, 32)

            @pl.when(to != me)
            def _():
                rcopy(msg.at[to], answers.at[me], ans_sem.at[0], ans_sem.at[1], dev(to)).start()

            return c

        return lax.fori_loop(0, 32, send, carry)

    lax.fori_loop(0, 4, lookup, 0)
    own = pltpu.make_async_copy(msg.at[me], answers.at[me], loc_sem.at[0])
    own.start()
    own.wait()
    wa = rcopy(msg.at[pl.ds(0, 127)], answers.at[pl.ds(0, 127)], ans_sem.at[0], ans_sem.at[1], partner)
    wa.wait_recv()
    in_copies[4].wait()

    halves = answers[...].astype(F32)
    flat = jnp.concatenate(
        [halves[:, 0:8].reshape(SLOTS, 128), halves[:, 8:16].reshape(SLOTS, 128)], axis=1
    ).astype(BF16)
    lane_e = lax.broadcasted_iota(I32, (LEN, 128), 1)
    x = dot(place[...], flat)
    eb = eband[...]
    tail = ((eb == 2.0) & (lane_e < 64)) | ((eb == 3.0) & (lane_e >= 64) & (lane_e < 96))
    xm[:, 0:128] = jnp.where(eb == 0.0, x[:, 0:128], 0.0).astype(BF16)
    xm[:, 128:256] = jnp.where(eb == 0.0, x[:, 128:256], 0.0).astype(BF16)
    xm[:, 256:384] = jnp.where(eb == 1.0, x[:, 0:128], 0.0).astype(BF16)
    xm[:, 384:512] = jnp.where(tail, x[:, 0:128], 0.0).astype(BF16)

    def halo(i, src, dst):
        return rcopy(src, dst, halo_sem.at[2 * i], halo_sem.at[2 * i + 1], partner)

    hi, lo = slice(HALF, LEN), slice(0, HALF)
    e_hi = dot(xm[hi], pext[...]).astype(BF16)
    ehalo_s[...] = e_hi[HALF - 16 :]
    h_e = halo(0, ehalo_s, ehalo_r)
    h_e.start()
    e32[8 + HALF :] = e_hi.astype(F32)
    e_lo = dot(xm[lo], pext[...]).astype(BF16)
    e32[8 : 8 + HALF] = e_lo.astype(F32)

    def stack(part, src, dst, gap):
        base = 0 if part == "lo" else HALF
        for k in range(3):
            dst[base : base + HALF, k * CH : (k + 1) * CH] = src[
                base + (2 - k) * gap : base + (2 - k) * gap + HALF
            ].astype(BF16)

    first_core = s == 0

    def layer1(base):
        hid[...] = dot(estack[base : base + HALF], w1v[...]) + b1[...]

        def block(i, c):
            r0 = pl.multiple_of(i * BLK, BLK)
            h = hid[pl.ds(r0, BLK)]
            cen = h - row_mean(h)
            rs = lax.rsqrt(row_mean(cen * cen) + EPS)
            n = cen * rs
            act, slope = gelu_parts(n * g1[...] + o1[...])
            at = pl.ds(base + r0, BLK)
            norm1[at] = n
            slope1[at] = slope
            rstd1[at] = jnp.broadcast_to(rs, (BLK, 128))
            a32[pl.ds(base + r0 + 16, BLK)] = act.astype(BF16).astype(F32)
            return c

        lax.fori_loop(0, HALF // BLK, block, 0)

    in_copies[5].wait()
    stack("hi", e32, estack, STEP)
    layer1(HALF)
    ahalo_s[...] = a32[LEN:].astype(BF16)
    h_a = halo(1, ahalo_s, ahalo_r)
    h_a.start()
    h_e.wait_recv()
    e32[0:8] = jnp.where(first_core, 0.0, ehalo_r[...].astype(F32)[8:16])
    stack("lo", e32, estack, STEP)
    layer1(0)

    in_copies[6].wait()
    in_copies[7].wait()
    zero8 = jnp.zeros((8, CH), F32)

    def layer2(base, sums):
        hid[...] = dot(astack[base : base + HALF], w2v[...]) + b2[...]

        def block(i, c):
            r0 = pl.multiple_of(i * BLK, BLK)
            h = hid[pl.ds(r0, BLK)]
            cen = h - row_mean(h)
            rs = lax.rsqrt(row_mean(cen * cen) + EPS)
            n = cen * rs
            act, slope = gelu_parts(n * g2[...] + o2[...])
            at = pl.ds(base + r0, BLK)
            bov[at] = (e32[pl.ds(base + r0 + 8, BLK)] + act).astype(BF16)
            du = ogv[at].astype(F32) * slope
            dn = du * g2[...]
            dh = (rs * (dn - row_mean(dn) - n * row_mean(dn * n))).astype(BF16).astype(F32)
            g2f[at] = dh
            return (c[0] + fold(dh), c[1] + fold(du * n), c[2] + fold(du))

        return lax.fori_loop(0, HALF // BLK, block, sums)

    stack("hi", a32, astack, 2 * STEP)
    sums2 = layer2(HALF, (zero8, zero8, zero8))
    h_a.wait_recv()
    a32[0:16] = jnp.where(first_core, 0.0, ahalo_r[...].astype(F32))
    stack("lo", a32, astack, 2 * STEP)
    sums2 = layer2(0, sums2)
    ghalo2_s[...] = g2f[0:16].astype(BF16)
    h_g2 = halo(2, ghalo2_s, ghalo2_r)
    h_g2.start()
    out_bo = pltpu.make_async_copy(bov, block_out, out_sem.at[0])
    out_bo.start()

    owns, xss, xrs, us = (own_a, own_b, own_c), (xs_a, xs_b, xs_c), (xr_a, xr_b, xr_c), (u_a, u_b, u_c)

    def core_copy(g):
        return rcopy(xss[g], xrs[g], core_sem.at[2 * g], core_sem.at[2 * g + 1], partner)

    def parts_of(g):
        return (3 * g, 3 * g + 1, 3 * g + 2) if g < 2 else (6,)

    def order(p):
        k = p % 3
        return AXES[k], AXES[(k + 1) % 3], AXES[(k + 2) % 3]

    def sems(p, stage):
        return ar_sem.at[p * 10 + 2 * stage], ar_sem.at[p * 10 + 2 * stage + 1]

    def home(p):
        g = min(p // 3, 2)
        return pl.multiple_of(BASES[g] + s * SPANS[g] + (p - 3 * g) * 256, 256)

    def wait3(p, stage, ref):
        send, recv = sems(p, stage)
        rcopy(ref, ref, send, recv, partner).wait_recv()

    def wait3_send(p, stage, ref):
        send, recv = sems(p, stage)
        rcopy(ref, ref, send, recv, partner).wait_send()

    def ar_stage0(g):
        core_copy(g).wait_recv()
        us[g][...] = (owns[g][...] + xrs[g][...].astype(F32)).astype(BF16)
        for p in parts_of(g):
            a = order(p)[0]
            send, recv = sems(p, 0)
            for j in (1, 2, 3):
                n, to = peer(a, j)
                off = pl.multiple_of((p - 3 * g) * 256 + n * 64, 64)
                rcopy(us[g].at[pl.ds(off, 64)], s1_r.at[p, j - 1], send, recv, to).start()

    def ar_stage1(g):
        for p in parts_of(g):
            a, b, _ = order(p)
            wait3(p, 0, s1_r.at[p])
            off = pl.multiple_of((p - 3 * g) * 256 + coord[a] * 64, 64)
            v = us[g][pl.ds(off, 64)].astype(F32)
            for j in range(3):
                v = v + s1_r[p, j].astype(F32)
            s2_s[p] = v.astype(BF16)
            send, recv = sems(p, 1)
            for j in (1, 2, 3):
                n, to = peer(b, j)
                rcopy(
                    s2_s.at[p, pl.ds(pl.multiple_of(n * 16, 16), 16)], s2_r.at[p, j - 1], send, recv, to
                ).start()

    def ar_stage2(g):
        for p in parts_of(g):
            _, b, c = order(p)
            wait3(p, 1, s2_r.at[p])
            v = s2_s[p, pl.ds(pl.multiple_of(coord[b] * 16, 16), 16)].astype(F32)
            for j in range(3):
                v = v + s2_r[p, j].astype(F32)
            s3_q[p, coord[c]] = v.astype(BF16)
            send, recv = sems(p, 2)
            for j in (1, 2, 3):
                _, to = peer(c, j)
                rcopy(s3_q.at[p, coord[c]], s3_q.at[p, coord[c]], send, recv, to).start()

    def ar_stage3(g):
        for p in parts_of(g):
            a, b, c = order(p)
            wait3(p, 2, s3_q.at[p, pl.ds(0, 3)])
            q = s3_q[p].astype(F32)
            at = pl.ds(pl.multiple_of(home(p) + coord[a] * 64 + coord[b] * 16, 16), 16)
            zbuf[at] = (((q[0] + q[1]) + q[2]) + q[3]).astype(BF16)
            send, recv = sems(p, 3)
            for j in (1, 2, 3):
                _, to = peer(b, j)
                rcopy(zbuf.at[at], zbuf.at[at], send, recv, to).start()

    def ar_stage4(g):
        for p in parts_of(g):
            a, b, c = order(p)
            wait3(p, 3, zbuf.at[pl.ds(0, 48)])
            at = pl.ds(pl.multiple_of(home(p) + coord[a] * 64, 64), 64)
            send, recv = sems(p, 4)
            for j in (1, 2, 3):
                _, to = peer(a, j)
                rcopy(zbuf.at[at], zbuf.at[at], send, recv, to).start()

    def ar_stage5(g):
        for p in parts_of(g):
            wait3(p, 4, zbuf.at[pl.ds(0, 192)])
            at = pl.ds(home(p), 256)
            rcopy(zbuf.at[at], zbuf.at[at], fin_sem.at[2 * p], fin_sem.at[2 * p + 1], partner).start()

    def ar_finish(g):
        for p in parts_of(g):
            at = pl.ds(home(p), 256)
            rcopy(zbuf.at[at], zbuf.at[at], fin_sem.at[2 * p], fin_sem.at[2 * p + 1], partner).wait()

    def ar_drain(g):
        core_copy(g).wait_send()
        for p in parts_of(g):
            wait3_send(p, 0, s1_r.at[p])
            wait3_send(p, 1, s2_r.at[p])
            wait3_send(p, 2, s3_q.at[p, pl.ds(0, 3)])
            wait3_send(p, 3, zbuf.at[pl.ds(0, 48)])
            wait3_send(p, 4, zbuf.at[pl.ds(0, 192)])

    def weight_sum(g, taps, gb):
        theirs = pl.ds(pl.multiple_of(other * 768, 256), 768)
        mine = pl.ds(pl.multiple_of(s * 768, 256), 768)
        xss[g][...] = dot(taps[:, theirs], gb, TN).astype(BF16)
        core_copy(g).start()
        owns[g][...] = dot(taps[:, mine], gb, TN)

    weight_sum(0, astack, g2f[0:LEN].astype(BF16))

    def back1(base, sums):
        hid[...] = sum(
            dot(g2f[base + k * 8 : base + k * 8 + HALF].astype(BF16), w2v[k * CH : (k + 1) * CH], NT)
            for k in range(3)
        )

        def block(i, c):
            r0 = pl.multiple_of(i * BLK, BLK)
            at = pl.ds(base + r0, BLK)
            n = norm1[at]
            du = hid[pl.ds(r0, BLK)] * slope1[at]
            dn = du * g1[...]
            rs = rstd1[at][:, 0:1]
            dh = (rs * (dn - row_mean(dn) - n * row_mean(dn * n))).astype(BF16).astype(F32)
            g1f[at] = dh
            return (c[0] + fold(dh), c[1] + fold(du * n), c[2] + fold(du))

        return lax.fori_loop(0, HALF // BLK, block, sums)

    sums1 = back1(0, (zero8, zero8, zero8))
    ghalo1_s[...] = g1f[0:16].astype(BF16)
    h_g1 = halo(3, ghalo1_s, ghalo1_r)
    h_g1.start()
    ar_stage0(0)
    h_g2.wait_recv()
    g2f[LEN:] = jnp.where(first_core, ghalo2_r[...].astype(F32), 0.0)
    sums1 = back1(HALF, sums1)
    ar_stage1(0)
    weight_sum(1, estack, g1f[0:LEN].astype(BF16))
    h_g1.wait_recv()
    g1f[LEN:] = jnp.where(first_core, ghalo1_r[...].astype(F32)[0:8], 0.0)
    ar_stage2(0)

    for base in (0, HALF):
        ge[base : base + HALF] = (
            ogv[base : base + HALF].astype(F32)
            + sum(
                dot(g1f[base + k * 4 : base + k * 4 + HALF].astype(BF16), w1v[k * CH : (k + 1) * CH], NT)
                for k in range(3)
            )
        ).astype(BF16)
    rg = dot(ge[...], pext[...], NT)
    first = jnp.where(eb == 0.0, rg[:, 0:128], jnp.where(eb == 1.0, rg[:, 256:384], rg[:, 384:512]))
    rgb = jnp.concatenate([first, rg[:, 128:256]], axis=1).astype(BF16)
    slots = dot(place[...], rgb, TN)
    gmsg[...] = jnp.concatenate(
        [slots[:, 0:128].reshape(NDEV, 8, 128), slots[:, 128:256].reshape(NDEV, 8, 128)], axis=1
    ).astype(BF16)

    def send_grad(k, c):
        to = lax.rem(me + k, NDEV)
        rcopy(gmsg.at[to], gotg.at[me], gr_sem.at[0], gr_sem.at[1], dev(to)).start()
        return c

    ar_stage0(1)
    lax.fori_loop(1, NDEV, send_grad, 0)
    own = pltpu.make_async_copy(gmsg.at[me], gotg.at[me], loc_sem.at[0])
    own.start()

    pg = dot(xm[...], ge[...], TN)
    owns_full = hid
    vec = jnp.concatenate(
        [jnp.sum(v, axis=0, keepdims=True) for v in (*sums1, *sums2)] + [jnp.zeros((2, CH), F32)], axis=0
    )
    own_c[...] = pg
    own_c[480:488] = vec
    xs_c[...] = own_c[pl.ds(pl.multiple_of(other * 256, 256), 256)].astype(BF16)
    core_copy(2).start()
    ar_stage3(0)
    ar_stage1(1)

    core_copy(2).wait_recv()
    u_c[...] = (own_c[pl.ds(pl.multiple_of(s * 256, 256), 256)] + xr_c[...].astype(F32)).astype(BF16)
    a6 = order(6)[0]
    for j in (1, 2, 3):
        n, to = peer(a6, j)
        send, recv = sems(6, 0)
        rcopy(u_c.at[pl.ds(pl.multiple_of(n * 64, 64), 64)], s1_r.at[6, j - 1], send, recv, to).start()
    ar_stage4(0)
    ar_stage2(1)
    ar_stage1(2)
    ar_stage5(0)
    ar_stage3(1)
    ar_stage2(2)
    ar_stage4(1)
    ar_stage3(2)

    own.wait()
    wg = rcopy(gmsg.at[pl.ds(0, 127)], gotg.at[pl.ds(0, 127)], gr_sem.at[0], gr_sem.at[1], partner)
    wg.wait_recv()
    band = code_sc[...] >> 11
    lane_s = lax.broadcasted_iota(I32, (SLOTS, 128), 1)
    both = gotg[...].astype(F32)
    h0, h1 = both[:, 0:8].reshape(SLOTS, 128), both[:, 8:16].reshape(SLOTS, 128)
    tail = ((band == 2) & (lane_s < 64)) | ((band == 3) & (lane_s >= 64) & (lane_s < 96))
    mt[0:128] = jnp.where(band == 0, h0, 0.0).T.astype(BF16)
    mt[128:256] = jnp.where(band == 0, h1, 0.0).T.astype(BF16)
    mt[256:384] = jnp.where(band == 1, h0, 0.0).T.astype(BF16)
    mt[384:512] = jnp.where(tail, h0, 0.0).T.astype(BF16)
    for b in range(4):
        tout[:, b * 512 : (b + 1) * 512] = dot(mt[...], onehot[:, b * 512 : (b + 1) * 512]).astype(BF16)
    outs = [
        (tout.at[0:256], t_wide), (tout.at[256:384], t_mid),
        (tout.at[384:448], t_narrow), (tout.at[448:480], t_thin),
    ]
    out_copies = [pltpu.make_async_copy(a, b, out_sem.at[1 + i]) for i, (a, b) in enumerate(outs)]
    for c in out_copies:
        c.start()

    ar_stage5(1)
    ar_stage4(2)
    ar_stage5(2)
    for g in range(3):
        ar_finish(g)
    out_z = pltpu.make_async_copy(zbuf, grads, out_sem.at[5])
    out_z.start()
    for g in range(3):
        ar_drain(g)
    rcopy(relay.at[pl.ds(0, 7)], relay.at[pl.ds(0, 7)], rq_sem.at[0], rq_sem.at[1], partner).wait_send()
    w2nd.wait_send()
    wa.wait_send()
    wg.wait_send()
    for h in (h_e, h_a, h_g2, h_g1):
        h.wait_send()
    out_bo.wait()
    for c in out_copies:
        c.wait()
    out_z.wait()


def scratch():
    v = pltpu.VMEM
    dma = pltpu.SemaphoreType.DMA
    return [
        v((512, ROWS), BF16), v((512, CH), BF16), v((1536, CH), BF16), v((1536, CH), BF16), v((LEN, CH), BF16),
        v((8, 16, 1, 128), I32), v((16, 8, 1, 128), I32), v((SLOTS, 128), I32), v((SLOTS, ROWS), BF16),
        v((LEN, SLOTS), BF16), v((NDEV, 16, 128), BF16), v((NDEV, 16, 128), BF16),
        v((LEN, 128), F32), v((LEN, 512), BF16), v((8 + LEN, CH), F32), v((16, CH), BF16), v((16, CH), BF16),
        v((LEN, 1536), BF16), v((HALF, CH), F32), v((LEN, CH), F32), v((LEN, CH), F32), v((LEN, 128), F32),
        v((16 + LEN, CH), F32), v((16, CH), BF16), v((16, CH), BF16), v((LEN, 1536), BF16),
        v((LEN, CH), BF16), v((LEN + 16, CH), F32), v((16, CH), BF16), v((16, CH), BF16),
        v((LEN + 8, CH), F32), v((16, CH), BF16), v((16, CH), BF16), v((LEN, CH), BF16),
        v((NDEV, 16, 128), BF16), v((NDEV, 16, 128), BF16), v((512, SLOTS), BF16), v((512, ROWS), BF16),
        v((768, CH), F32), v((768, CH), F32), v((512, CH), F32),
        v((768, CH), BF16), v((768, CH), BF16), v((256, CH), BF16),
        v((768, CH), BF16), v((768, CH), BF16), v((256, CH), BF16),
        v((768, CH), BF16), v((768, CH), BF16), v((256, CH), BF16),
        v((7, 3, 64, CH), BF16), v((7, 64, CH), BF16), v((7, 3, 16, CH), BF16), v((7, 4, 16, CH), BF16),
        v((3584, CH), BF16),
        dma((8,)), dma((4,)), dma((2,)), dma((8,)), dma((2,)), dma((6,)), dma((70,)), dma((14,)), dma((6,)), dma((1,)),
    ]


def shards(
    table_wide, table_mid, table_narrow, table_thin, band_proj, first_conv_weight, first_conv_bias,
    gain_first, offset_first, second_conv_weight, second_conv_bias, gain_second, offset_second,
    slot_event, slot_counts, slot_band, slot_row, out_grad,
):
    live = jnp.arange(CAP, dtype=I32)[None, :] < slot_counts[0, 0][:, None]
    code = slot_row[0, 0] + ROWS * slot_band[0, 0]
    codes = jnp.pad(code, ((0, 0), (0, 128 - CAP))).reshape(16, 8, 1, 128)
    target = jnp.where(live, slot_event[0, 0], LEN).reshape(1, SLOTS)
    sband = slot_band[0, 0].reshape(1, SLOTS)
    vecs = [
        v.reshape(1, CH)
        for v in (first_conv_bias, gain_first, offset_first, second_conv_bias, gain_second, offset_second)
    ]
    hbm, vmem = pl.BlockSpec(memory_space=pl.ANY), pl.BlockSpec(memory_space=pltpu.VMEM)
    sds = jax.ShapeDtypeStruct
    block_out, tw, tm, tn, tt, grads = pl.pallas_call(
        kernel,
        out_shape=[
            sds((LEN, CH), BF16), sds((256, ROWS), BF16), sds((128, ROWS), BF16), sds((64, ROWS), BF16),
            sds((32, ROWS), BF16), sds((3584, CH), BF16),
        ],
        in_specs=[hbm] * 8 + [vmem] * 9,
        out_specs=[hbm] * 6,
        scratch_shapes=scratch(),
        compiler_params=pltpu.CompilerParams(
            collective_id=0, has_side_effects=True, vmem_limit_bytes=60 << 20
        ),
        cost_estimate=pl.CostEstimate(flops=12 * 10**9, bytes_accessed=14 * 2**20, transcendentals=2**19),
    )(
        table_wide, table_mid, table_narrow, table_thin, band_proj, first_conv_weight, second_conv_weight,
        out_grad[0], codes, target, sband, *vecs,
    )
    scale = 1.0 / float(NDEV * LEN) ** 0.5
    wide_grads = grads.astype(F32) * scale
    return (
        block_out[None], tw, tm, tn, tt, wide_grads[3072:3552], wide_grads[1536:3072], wide_grads[0:1536],
        wide_grads[3552:3558],
    )


def solution(mesh):
    rows = P(None, ("table", "seq", "dp"))
    hist = ("table", "dp")
    in_specs = (rows,) * 4 + (P(),) * 9 + (
        P(hist, "seq", None, None), P(hist, "seq", None), P(hist, "seq", None, None), P(hist, "seq", None, None),
        P(hist, "seq", None),
    )
    out_specs = (P(hist, "seq", None),) + (rows,) * 4 + (P(),) * 4
    return jax.shard_map(shards, mesh=mesh, in_specs=in_specs, out_specs=out_specs, check_vma=False)
```

```python
import jax
import jax.numpy as jnp
from jax import lax
from jax.experimental import pallas as pl
from jax.experimental.pallas import tpu as pltpu
from jax.sharding import PartitionSpec as P

MESH = pl.DeviceIdType.MESH
F32, BF16, I32 = jnp.float32, jnp.bfloat16, jnp.int32
STEP = 4
EPS = 1e-5
NDEV, CAP, SLOTS, LEN, CH, ROWS = 128, 8, 1024, 512, 512, 2048
HALF = 256
BLK = 128
GC = 0.7978845608028654
GA = 0.044715
NT = (((1,), (1,)), ((), ()))
TN = (((0,), (0,)), ((), ()))
BASES = (0, 1536, 3072)
SPANS = (768, 768, 256)
AXES = ("x", "y", "z")


def dot(a, b, dims=None):
    if dims is None:
        return jnp.dot(a, b, preferred_element_type=F32)
    return lax.dot_general(a, b, dims, preferred_element_type=F32)


def gelu_parts(u):
    sq = u * u
    t = jnp.tanh(GC * (u + GA * u * sq))
    half = 0.5 * (1.0 + t)
    slope = half + (0.5 * GC) * u * (1.0 - t * t) * (1.0 + (3.0 * GA) * sq)
    return u * half, slope


def row_mean(v):
    return jnp.sum(v, axis=-1, keepdims=True) * (1.0 / CH)


def fold(v):
    return jnp.sum(v.reshape(v.shape[0] // 8, 8, v.shape[1]), axis=0)


def picked_lane(v, by_row):
    lane = lax.broadcasted_iota(I32, (NDEV, CAP, 128), 2)
    want = lax.broadcasted_iota(I32, (NDEV, CAP, 128), 1 if by_row else 0)
    if not by_row:
        want = want % 8
    one = jnp.sum(jnp.where(lane == want, v, 0.0), axis=-1, keepdims=True)
    return jnp.broadcast_to(one, (NDEV, CAP, 128)).reshape(SLOTS, 128)


def spread(v):
    return picked_lane(jnp.broadcast_to(v, (NDEV, CAP, 128)), 1)


def turned(v):
    full = jnp.concatenate([v, jnp.zeros((120, 128), F32)], axis=0)
    return full.T


def kernel(
    wide, mid, narrow, thin, proj, w1, w2, og,
    srow, sbandr, sevent, scount, b1, g1, o1, b2, g2, o2,
    block_out, t_wide, t_mid, t_narrow, t_thin, grads,
    tcat, pext, w1v, w2v, ogv, codes, relay, passed, fetched, code_sc, onehot, place, xin, msg, answers,
    eband, xm, e32, ehalo_s, ehalo_r, estack, hid, norm1, slope1, rstd1, a32, ahalo_s, ahalo_r, astack,
    bov, g2f, ghalo2_s, ghalo2_r, g1f, ghalo1_s, ghalo1_r, ge, gmsg, gotg, mt, tout,
    own_a, own_b, own_c, xs_a, xs_b, xs_c, xr_a, xr_b, xr_c, u_a, u_b, u_c,
    s1_r, s2_s, s2_r, s3_q, c1_r, c2_s, c2_r, c3_q, zbuf,
    in_sem, rq_sem, ans_sem, halo_sem, gr_sem, core_sem, ar_sem, fin_sem, out_sem, loc_sem,
):
    t, s, d = lax.axis_index("table"), lax.axis_index("seq"), lax.axis_index("dp")
    sd = s * 4 + d
    me = t * 8 + sd
    coord = {"x": lax.rem(t, 4), "y": d, "z": t // 4}
    other = 1 - s

    def peer(axis, j):
        n = lax.rem(coord[axis] + j, 4)
        if axis == "x":
            return n, (t - coord["x"] + n, s, d)
        if axis == "y":
            return n, (t, s, n)
        return n, (n * 4 + coord["x"], s, d)

    def dev(o):
        return (o // 8, lax.rem(o // 4, 2), lax.rem(o, 4))

    def rcopy(src, dst, send, recv, to):
        return pltpu.make_async_remote_copy(
            src_ref=src, dst_ref=dst, send_sem=send, recv_sem=recv, device_id=to, device_id_type=MESH
        )

    partner = (t, other, d)

    ins = [
        (wide, tcat.at[0:256]), (mid, tcat.at[256:384]), (narrow, tcat.at[384:448]),
        (thin, tcat.at[448:480]), (proj, pext.at[0:480]), (w1, w1v), (w2, w2v), (og, ogv),
    ]
    in_copies = [pltpu.make_async_copy(a, b, in_sem.at[i]) for i, (a, b) in enumerate(ins)]
    for c in in_copies:
        c.start()

    code_t = turned((srow[...] + ROWS * sbandr[...]).astype(F32)).reshape(16, 8, 128)
    asked = code_t[0]
    for k in range(1, 16):
        asked = asked + pltpu.roll(code_t[k], k * 8, 1)
    codes[...] = asked.astype(I32).reshape(8, 1, 128)

    pending = list(c.wait for c in in_copies)

    def finish():
        for f in pending:
            f()

    bar = pltpu.get_barrier_semaphore()

    def near(k):
        n = lax.rem(sd + k, 8)
        return n, (t, n // 4, lax.rem(n, 4))

    def far(k):
        n = lax.rem(t + k, 16)
        return n, (n, s, d)

    def sig_near(k, c):
        pl.semaphore_signal(bar, inc=1, device_id=near(k)[1], device_id_type=MESH)
        return c

    def sig_far(k, c):
        pl.semaphore_signal(bar, inc=1, device_id=far(k)[1], device_id_type=MESH)
        return c

    lax.fori_loop(1, 8, sig_near, 0)
    lax.fori_loop(1, 16, sig_far, 0)
    pl.semaphore_wait(bar, 22)

    def ask_near(k, c):
        n, to = near(k)
        rcopy(codes.at[n], relay.at[sd], rq_sem.at[0], rq_sem.at[1], to).start()
        return c

    lax.fori_loop(1, 8, ask_near, 0)
    relay[sd] = codes[sd]
    pext[480:512] = jnp.zeros((32, CH), BF16)
    tcat[480:512] = jnp.zeros((32, ROWS), BF16)

    w = rcopy(relay.at[pl.ds(0, 7)], relay.at[pl.ds(0, 7)], rq_sem.at[0], rq_sem.at[1], partner)
    w.wait_recv()
    pending.append(w.wait_send)

    passed[...] = turned(relay[...].reshape(8, 128).astype(F32)).astype(I32).reshape(16, 8, 128)

    def ask_far(k, c):
        n, to = far(k)
        rcopy(passed.at[n], fetched.at[t], rq_sem.at[2], rq_sem.at[3], to).start()
        return c

    lax.fori_loop(1, 16, ask_far, 0)
    fetched[t] = passed[t]
    w2nd = rcopy(fetched.at[pl.ds(0, 15)], fetched.at[pl.ds(0, 15)], rq_sem.at[2], rq_sem.at[3], partner)
    w2nd.wait_recv()
    pending.append(w2nd.wait_send)

    wide_f = jnp.broadcast_to(fetched[...].astype(F32).reshape(16, 1, 8, 128), (16, 8, 8, 128))
    code_sc[...] = picked_lane(wide_f.reshape(NDEV, CAP, 128), 0).astype(I32)

    for c in in_copies[:4]:
        c.wait()
    del pending[:4]

    lane128 = lax.broadcasted_iota(I32, (HALF, 128), 1)

    def lookup(i, carry):
        cb = lax.rem(me // 32 + i, 4)
        rows = pl.ds(pl.multiple_of(cb * HALF, HALF), HALF)
        code = code_sc[rows]
        row, band = code & (ROWS - 1), code >> 11
        for b in range(ROWS // 128):
            onehot[rows, b * 128 : (b + 1) * 128] = (row == lane128 + b * 128).astype(F32).astype(BF16)
        got_rows = dot(onehot[rows], tcat[...], NT)
        first = jnp.where(
            band == 0, got_rows[:, 0:128], jnp.where(band == 1, got_rows[:, 256:384], got_rows[:, 384:512])
        )
        both = jnp.concatenate(
            [first.reshape(32, 8, 128), got_rows[:, 128:256].reshape(32, 8, 128)], axis=1
        )
        msg[pl.ds(cb * 32, 32)] = both.astype(BF16)

        def send(k, c):
            to = cb * 32 + lax.rem(me + k, 32)

            @pl.when(to != me)
            def _():
                rcopy(msg.at[to], answers.at[me], ans_sem.at[0], ans_sem.at[1], dev(to)).start()

            return c

        return lax.fori_loop(0, 32, send, carry)

    lax.fori_loop(0, 4, lookup, 0)

    live = lax.broadcasted_iota(I32, (CAP, NDEV), 0) < scount[...]
    target = spread(turned(jnp.where(live, sevent[...], LEN).astype(F32)).reshape(NDEV, 1, 128)).astype(I32)
    lane_p = lax.broadcasted_iota(I32, (SLOTS, 128), 1)
    for b in range(4):
        place[:, b * 128 : (b + 1) * 128] = (target == lane_p + b * 128).astype(F32).astype(BF16)
    xin[:, 256:384] = spread(turned(sbandr[...].astype(F32)).reshape(NDEV, 1, 128)).astype(BF16)
    own = pltpu.make_async_copy(msg.at[me], answers.at[me], loc_sem.at[0])
    own.start()
    own.wait()
    wa = rcopy(msg.at[pl.ds(0, 127)], answers.at[pl.ds(0, 127)], ans_sem.at[0], ans_sem.at[1], partner)
    wa.wait_recv()
    pending.append(wa.wait_send)
    in_copies[4].wait()
    del pending[0]

    halves = answers[...].astype(F32)
    xin[:, 0:128] = halves[:, 0:8].reshape(SLOTS, 128).astype(BF16)
    xin[:, 128:256] = halves[:, 8:16].reshape(SLOTS, 128).astype(BF16)
    lane_e = lax.broadcasted_iota(I32, (LEN, 128), 1)
    x = dot(place[...], xin[...], TN)
    eb = x[:, 256:384]
    eband[...] = eb
    tail = ((eb == 2.0) & (lane_e < 64)) | ((eb == 3.0) & (lane_e >= 64) & (lane_e < 96))
    xm[:, 0:128] = jnp.where(eb == 0.0, x[:, 0:128], 0.0).astype(BF16)
    xm[:, 128:256] = jnp.where(eb == 0.0, x[:, 128:256], 0.0).astype(BF16)
    xm[:, 256:384] = jnp.where(eb == 1.0, x[:, 0:128], 0.0).astype(BF16)
    xm[:, 384:512] = jnp.where(tail, x[:, 0:128], 0.0).astype(BF16)

    def halo(i, src, dst):
        return rcopy(src, dst, halo_sem.at[2 * i], halo_sem.at[2 * i + 1], partner)

    hi, lo = slice(HALF, LEN), slice(0, HALF)
    e_hi = dot(xm[hi], pext[...]).astype(BF16)
    ehalo_s[...] = e_hi[HALF - 16 :]
    h_e = halo(0, ehalo_s, ehalo_r)
    h_e.start()
    e32[8 + HALF :] = e_hi.astype(F32)
    e_lo = dot(xm[lo], pext[...]).astype(BF16)
    e32[8 : 8 + HALF] = e_lo.astype(F32)

    def stack(part, src, dst, gap):
        base = 0 if part == "lo" else HALF
        for k in range(3):
            dst[base : base + HALF, k * CH : (k + 1) * CH] = src[
                base + (2 - k) * gap : base + (2 - k) * gap + HALF
            ].astype(BF16)

    first_core = s == 0

    def layer1(base):
        hid[...] = dot(estack[base : base + HALF], w1v[...]) + b1[...]

        def block(i, c):
            r0 = pl.multiple_of(i * BLK, BLK)
            h = hid[pl.ds(r0, BLK)]
            cen = h - row_mean(h)
            rs = lax.rsqrt(row_mean(cen * cen) + EPS)
            n = cen * rs
            act, slope = gelu_parts(n * g1[...] + o1[...])
            at = pl.ds(base + r0, BLK)
            norm1[at] = n
            slope1[at] = slope
            rstd1[at] = jnp.broadcast_to(rs, (BLK, 128))
            a32[pl.ds(base + r0 + 16, BLK)] = act.astype(BF16).astype(F32)
            return c

        lax.fori_loop(0, HALF // BLK, block, 0)

    pending.append(h_e.wait_send)
    in_copies[5].wait()
    del pending[0]
    stack("hi", e32, estack, STEP)
    layer1(HALF)
    ahalo_s[...] = a32[LEN:].astype(BF16)
    h_a = halo(1, ahalo_s, ahalo_r)
    h_a.start()
    h_e.wait_recv()
    e32[0:8] = jnp.where(first_core, 0.0, ehalo_r[...].astype(F32)[8:16])
    stack("lo", e32, estack, STEP)
    layer1(0)

    pending.append(h_a.wait_send)
    in_copies[6].wait()
    in_copies[7].wait()
    del pending[:2]
    zero8 = jnp.zeros((8, CH), F32)

    def layer2(base, sums):
        hid[...] = dot(astack[base : base + HALF], w2v[...]) + b2[...]

        def block(i, c):
            r0 = pl.multiple_of(i * BLK, BLK)
            h = hid[pl.ds(r0, BLK)]
            cen = h - row_mean(h)
            rs = lax.rsqrt(row_mean(cen * cen) + EPS)
            n = cen * rs
            act, slope = gelu_parts(n * g2[...] + o2[...])
            at = pl.ds(base + r0, BLK)
            bov[at] = (e32[pl.ds(base + r0 + 8, BLK)] + act).astype(BF16)
            du = ogv[at].astype(F32) * slope
            dn = du * g2[...]
            dh = (rs * (dn - row_mean(dn) - n * row_mean(dn * n))).astype(BF16).astype(F32)
            g2f[at] = dh
            return (c[0] + fold(dh), c[1] + fold(du * n), c[2] + fold(du))

        return lax.fori_loop(0, HALF // BLK, block, sums)

    stack("hi", a32, astack, 2 * STEP)
    sums2 = layer2(HALF, (zero8, zero8, zero8))
    h_a.wait_recv()
    a32[0:16] = jnp.where(first_core, 0.0, ahalo_r[...].astype(F32))
    stack("lo", a32, astack, 2 * STEP)
    sums2 = layer2(0, sums2)
    ghalo2_s[...] = g2f[0:16].astype(BF16)
    h_g2 = halo(2, ghalo2_s, ghalo2_r)
    h_g2.start()
    out_bo = pltpu.make_async_copy(bov, block_out, out_sem.at[0])
    out_bo.start()
    pending += [h_g2.wait_send, out_bo.wait]

    owns, xss, xrs, us = (own_a, own_b, own_c), (xs_a, xs_b, xs_c), (xr_a, xr_b, xr_c), (u_a, u_b, u_c)

    def core_copy(g):
        return rcopy(xss[g], xrs[g], core_sem.at[2 * g], core_sem.at[2 * g + 1], partner)

    def parts_of(g):
        return (3 * g, 3 * g + 1, 3 * g + 2) if g < 2 else (6, 7)

    def first_row(p):
        return (p - 3 * min(p // 3, 2)) * (256 if p < 6 else 128)

    def order(p):
        k = (p + (p >= 6)) % 3
        return AXES[k], AXES[(k + 1) % 3], AXES[(k + 2) % 3]

    def sems(p, stage):
        return ar_sem.at[p * 10 + 2 * stage], ar_sem.at[p * 10 + 2 * stage + 1]

    def home(p):
        g = min(p // 3, 2)
        return pl.multiple_of(BASES[g] + s * SPANS[g] + first_row(p), 128)

    def chunk_rows(p):
        return 64 if p < 6 else 32

    def cut1(p, n):
        c = chunk_rows(p)
        return pl.ds(pl.multiple_of(first_row(p) + n * c, c), c)

    def cut2(ref, n):
        if ref.shape[0] == 64:
            return ref.at[pl.ds(pl.multiple_of(n * 16, 16), 16)]
        return ref.at[:, pl.ds(pl.multiple_of(n * 128, 128), 128)]

    def bufs(p):
        i = p if p < 6 else p - 6
        return tuple(r.at[i] for r in ((s1_r, s2_s, s2_r, s3_q) if p < 6 else (c1_r, c2_s, c2_r, c3_q)))

    def chunk_home(p, n):
        c = chunk_rows(p)
        return zbuf.at[pl.ds(pl.multiple_of(home(p) + n * c, c), c)]

    def last3(p, stage):
        if stage == 0:
            return bufs(p)[0]
        if stage == 1:
            return bufs(p)[2]
        if stage in (2, 3):
            return bufs(p)[3].at[pl.ds(0, 3)]
        return zbuf.at[pl.ds(0, 3 * chunk_rows(p))]

    def wait3(p, stage):
        send, recv = sems(p, stage)
        rcopy(last3(p, stage), last3(p, stage), send, recv, partner).wait_recv()
        pending.append(rcopy(last3(p, stage), last3(p, stage), send, recv, partner).wait_send)

    def ar_stage0(g):
        core_copy(g).wait_recv()
        pending.append(core_copy(g).wait_send)
        mine = owns[g][...] if g < 2 else own_c[pl.ds(pl.multiple_of(s * 256, 256), 256)]
        us[g][...] = (mine + xrs[g][...].astype(F32)).astype(BF16)
        for p in parts_of(g):
            send, recv = sems(p, 0)
            for j in (1, 2, 3):
                n, to = peer(order(p)[0], j)
                rcopy(us[g].at[cut1(p, n)], bufs(p)[0].at[j - 1], send, recv, to).start()

    def ar_stage1(g):
        for p in parts_of(g):
            a, b, _ = order(p)
            s1, s2s, s2r, _ = bufs(p)
            wait3(p, 0)
            v = us[g][cut1(p, coord[a])].astype(F32)
            for j in range(3):
                v = v + s1[j].astype(F32)
            s2s[...] = v.astype(BF16)
            send, recv = sems(p, 1)
            for j in (1, 2, 3):
                n, to = peer(b, j)
                rcopy(cut2(s2s, n), s2r.at[j - 1], send, recv, to).start()

    def ar_stage2(g):
        for p in parts_of(g):
            _, b, c = order(p)
            _, s2s, s2r, q = bufs(p)
            wait3(p, 1)
            v = cut2(s2s, coord[b])[...].astype(F32)
            for j in range(3):
                v = v + s2r[j].astype(F32)
            q[coord[c]] = v.astype(BF16)
            send, recv = sems(p, 2)
            for j in (1, 2, 3):
                _, to = peer(c, j)
                rcopy(q.at[coord[c]], q.at[coord[c]], send, recv, to).start()

    def ar_stage3(g):
        for p in parts_of(g):
            a, b, _ = order(p)
            wait3(p, 2)
            q = bufs(p)[3][...].astype(F32)
            to_ref = cut2(chunk_home(p, coord[a]), coord[b])
            to_ref[...] = (((q[0] + q[1]) + q[2]) + q[3]).astype(BF16)
            send, recv = sems(p, 3)
            for j in (1, 2, 3):
                _, to = peer(b, j)
                rcopy(to_ref, to_ref, send, recv, to).start()

    def ar_stage4(g):
        for p in parts_of(g):
            a = order(p)[0]
            wait3(p, 3)
            ref = chunk_home(p, coord[a])
            send, recv = sems(p, 4)
            for j in (1, 2, 3):
                _, to = peer(a, j)
                rcopy(ref, ref, send, recv, to).start()

    def last_copy(p):
        ref = zbuf.at[pl.ds(home(p), 4 * chunk_rows(p))]
        return rcopy(ref, ref, fin_sem.at[2 * p], fin_sem.at[2 * p + 1], partner)

    def ar_stage5(g):
        for p in parts_of(g):
            wait3(p, 4)
            last_copy(p).start()

    def ar_finish(g):
        for p in parts_of(g):
            last_copy(p).wait()
        at = pl.ds(BASES[g], 2 * SPANS[g])
        c = pltpu.make_async_copy(zbuf.at[at], grads.at[at], out_sem.at[5 + g])
        c.start()
        pending.append(c.wait)

    def weight_sum(g, taps, gb):
        theirs = pl.ds(pl.multiple_of(other * 768, 256), 768)
        mine = pl.ds(pl.multiple_of(s * 768, 256), 768)
        xss[g][...] = dot(taps[:, theirs], gb, TN).astype(BF16)
        core_copy(g).start()
        owns[g][...] = dot(taps[:, mine], gb, TN)

    weight_sum(0, astack, g2f[0:LEN].astype(BF16))

    def back1(base, sums):
        hid[...] = sum(
            dot(g2f[base + k * 8 : base + k * 8 + HALF].astype(BF16), w2v[k * CH : (k + 1) * CH], NT)
            for k in range(3)
        )

        def block(i, c):
            r0 = pl.multiple_of(i * BLK, BLK)
            at = pl.ds(base + r0, BLK)
            n = norm1[at]
            du = hid[pl.ds(r0, BLK)] * slope1[at]
            dn = du * g1[...]
            rs = rstd1[at][:, 0:1]
            dh = (rs * (dn - row_mean(dn) - n * row_mean(dn * n))).astype(BF16).astype(F32)
            g1f[at] = dh
            return (c[0] + fold(dh), c[1] + fold(du * n), c[2] + fold(du))

        return lax.fori_loop(0, HALF // BLK, block, sums)

    sums1 = back1(0, (zero8, zero8, zero8))
    ghalo1_s[...] = g1f[0:16].astype(BF16)
    h_g1 = halo(3, ghalo1_s, ghalo1_r)
    h_g1.start()
    pending.append(h_g1.wait_send)
    ar_stage0(0)
    h_g2.wait_recv()
    g2f[LEN:] = jnp.where(first_core, ghalo2_r[...].astype(F32), 0.0)
    sums1 = back1(HALF, sums1)
    weight_sum(1, estack, g1f[0:LEN].astype(BF16))
    h_g1.wait_recv()
    g1f[LEN:] = jnp.where(first_core, ghalo1_r[...].astype(F32)[0:8], 0.0)
    ar_stage1(0)
    ar_stage0(1)

    for base in (0, HALF):
        ge[base : base + HALF] = (
            ogv[base : base + HALF].astype(F32)
            + sum(
                dot(g1f[base + k * 4 : base + k * 4 + HALF].astype(BF16), w1v[k * CH : (k + 1) * CH], NT)
                for k in range(3)
            )
        ).astype(BF16)

    own_c[...] = dot(xm[...], ge[...], TN)
    own_c[480:488] = jnp.concatenate(
        [jnp.sum(v, axis=0, keepdims=True) for v in (*sums1, *sums2)] + [jnp.zeros((2, CH), F32)], axis=0
    )
    xs_c[...] = own_c[pl.ds(pl.multiple_of(other * 256, 256), 256)].astype(BF16)
    core_copy(2).start()
    ar_stage2(0)

    rg = dot(ge[...], pext[...], NT)
    first = jnp.where(eb == 0.0, rg[:, 0:128], jnp.where(eb == 1.0, rg[:, 256:384], rg[:, 384:512]))
    rgb = jnp.concatenate([first, rg[:, 128:256]], axis=1).astype(BF16)
    slots = dot(place[...], rgb)
    gmsg[...] = jnp.concatenate(
        [slots[:, 0:128].reshape(NDEV, 8, 128), slots[:, 128:256].reshape(NDEV, 8, 128)], axis=1
    ).astype(BF16)
    ar_stage0(2)

    def send_grad(k, c):
        to = lax.rem(me + k, NDEV)
        rcopy(gmsg.at[to], gotg.at[me], gr_sem.at[0], gr_sem.at[1], dev(to)).start()
        return c

    lax.fori_loop(1, 43, send_grad, 0)
    own = pltpu.make_async_copy(gmsg.at[me], gotg.at[me], loc_sem.at[0])
    own.start()
    ar_stage1(1)
    ar_stage3(0)
    lax.fori_loop(43, 86, send_grad, 0)
    ar_stage1(2)
    ar_stage2(1)
    lax.fori_loop(86, NDEV, send_grad, 0)
    ar_stage4(0)
    ar_stage2(2)
    ar_stage3(1)
    ar_stage3(2)
    ar_stage4(1)
    ar_stage5(0)
    ar_stage4(2)

    own.wait()
    wg = rcopy(gmsg.at[pl.ds(0, 127)], gotg.at[pl.ds(0, 127)], gr_sem.at[0], gr_sem.at[1], partner)
    wg.wait_recv()
    pending.append(wg.wait_send)
    ar_finish(0)
    band = code_sc[...] >> 11
    lane_s = lax.broadcasted_iota(I32, (SLOTS, 128), 1)
    both = gotg[...].astype(F32)
    h0, h1 = both[:, 0:8].reshape(SLOTS, 128), both[:, 8:16].reshape(SLOTS, 128)
    tail = ((band == 2) & (lane_s < 64)) | ((band == 3) & (lane_s >= 64) & (lane_s < 96))
    mt[0:128] = jnp.where(band == 0, h0, 0.0).T.astype(BF16)
    mt[128:256] = jnp.where(band == 0, h1, 0.0).T.astype(BF16)
    mt[256:384] = jnp.where(band == 1, h0, 0.0).T.astype(BF16)
    mt[384:512] = jnp.where(tail, h0, 0.0).T.astype(BF16)
    for b in range(4):
        tout[:, b * 512 : (b + 1) * 512] = dot(mt[...], onehot[:, b * 512 : (b + 1) * 512]).astype(BF16)
    outs = [
        (tout.at[0:256], t_wide), (tout.at[256:384], t_mid),
        (tout.at[384:448], t_narrow), (tout.at[448:480], t_thin),
    ]
    for i, (a, b) in enumerate(outs):
        c = pltpu.make_async_copy(a, b, out_sem.at[1 + i])
        c.start()
        pending.append(c.wait)

    ar_stage5(1)
    ar_stage5(2)
    ar_finish(1)
    ar_finish(2)
    finish()


def scratch():
    v = pltpu.VMEM
    dma = pltpu.SemaphoreType.DMA
    return [
        v((512, ROWS), BF16), v((512, CH), BF16), v((1536, CH), BF16), v((1536, CH), BF16), v((LEN, CH), BF16),
        v((8, 1, 128), I32), v((8, 1, 128), I32), v((16, 8, 128), I32), v((16, 8, 128), I32), v((SLOTS, 128), I32), v((SLOTS, ROWS), BF16),
        v((SLOTS, LEN), BF16), v((SLOTS, 384), BF16), v((NDEV, 16, 128), BF16), v((NDEV, 16, 128), BF16),
        v((LEN, 128), F32), v((LEN, 512), BF16), v((8 + LEN, CH), F32), v((16, CH), BF16), v((16, CH), BF16),
        v((LEN, 1536), BF16), v((HALF, CH), F32), v((LEN, CH), F32), v((LEN, CH), F32), v((LEN, 128), F32),
        v((16 + LEN, CH), F32), v((16, CH), BF16), v((16, CH), BF16), v((LEN, 1536), BF16),
        v((LEN, CH), BF16), v((LEN + 16, CH), F32), v((16, CH), BF16), v((16, CH), BF16),
        v((LEN + 8, CH), F32), v((16, CH), BF16), v((16, CH), BF16), v((LEN, CH), BF16),
        v((NDEV, 16, 128), BF16), v((NDEV, 16, 128), BF16), v((512, SLOTS), BF16), v((512, ROWS), BF16),
        v((768, CH), F32), v((768, CH), F32), v((512, CH), F32),
        v((768, CH), BF16), v((768, CH), BF16), v((256, CH), BF16),
        v((768, CH), BF16), v((768, CH), BF16), v((256, CH), BF16),
        v((768, CH), BF16), v((768, CH), BF16), v((256, CH), BF16),
        v((6, 3, 64, CH), BF16), v((6, 64, CH), BF16), v((6, 3, 16, CH), BF16), v((6, 4, 16, CH), BF16),
        v((2, 3, 32, CH), BF16), v((2, 32, CH), BF16), v((2, 3, 32, 128), BF16), v((2, 4, 32, 128), BF16),
        v((3584, CH), BF16),
        dma((8,)), dma((4,)), dma((2,)), dma((8,)), dma((2,)), dma((6,)), dma((80,)), dma((16,)), dma((8,)), dma((1,)),
    ]


def shards(
    table_wide, table_mid, table_narrow, table_thin, band_proj, first_conv_weight, first_conv_bias,
    gain_first, offset_first, second_conv_weight, second_conv_bias, gain_second, offset_second,
    slot_event, slot_counts, slot_band, slot_row, out_grad,
):
    across = [v[0, 0].T for v in (slot_row, slot_band, slot_event)]
    vecs = [
        v.reshape(1, CH)
        for v in (first_conv_bias, gain_first, offset_first, second_conv_bias, gain_second, offset_second)
    ]
    hbm, vmem = pl.BlockSpec(memory_space=pl.ANY), pl.BlockSpec(memory_space=pltpu.VMEM)
    sds = jax.ShapeDtypeStruct
    block_out, tw, tm, tn, tt, grads = pl.pallas_call(
        kernel,
        out_shape=[
            sds((LEN, CH), BF16), sds((256, ROWS), BF16), sds((128, ROWS), BF16), sds((64, ROWS), BF16),
            sds((32, ROWS), BF16), sds((3584, CH), BF16),
        ],
        in_specs=[hbm] * 8 + [vmem] * 10,
        out_specs=[hbm] * 6,
        scratch_shapes=scratch(),
        compiler_params=pltpu.CompilerParams(
            collective_id=0, has_side_effects=True, vmem_limit_bytes=60 << 20
        ),
        cost_estimate=pl.CostEstimate(flops=12 * 10**9, bytes_accessed=14 * 2**20, transcendentals=2**19),
    )(
        table_wide, table_mid, table_narrow, table_thin, band_proj, first_conv_weight, second_conv_weight,
        out_grad[0], *across, slot_counts[0], *vecs,
    )
    copied = [block_out, tw, tm, tn, tt]
    outs = pl.pallas_call(
        finish_kernel,
        out_shape=[sds(v.shape, v.dtype) for v in copied]
        + [sds((480, CH), F32), sds((1536, CH), F32), sds((1536, CH), F32), sds((6, CH), F32)],
        in_specs=[hbm] * 6,
        out_specs=[hbm] * 9,
        scratch_shapes=[pltpu.VMEM(v.shape, v.dtype) for v in copied]
        + [
            pltpu.VMEM((3584, CH), BF16), pltpu.VMEM((3584, CH), F32), pltpu.VMEM((6, CH), F32),
            pltpu.SemaphoreType.DMA((5,)), pltpu.SemaphoreType.DMA((7,)), pltpu.SemaphoreType.DMA((8,)), pltpu.SemaphoreType.DMA((5,)),
        ],
        compiler_params=pltpu.CompilerParams(vmem_limit_bytes=60 << 20),
    )(*copied, grads)
    return (outs[0][None], *outs[1:])


def finish_kernel(*refs):
    copied, z, outs = refs[:5], refs[5], refs[6:15]
    held = refs[15:20]
    zb, zf, vec, cs, zs, os_, ds = refs[20:]
    loads = [
        pltpu.make_async_copy(z.at[i * 512 : (i + 1) * 512], zb.at[i * 512 : (i + 1) * 512], zs.at[i])
        for i in range(7)
    ]
    arrivals = [pltpu.make_async_copy(a, b, cs.at[i]) for i, (a, b) in enumerate(zip(copied, held))]
    for c in loads[:4] + arrivals + loads[4:]:
        c.start()
    moves = []
    scale = 1.0 / float(NDEV * LEN) ** 0.5
    proj, c1, c2, vout = outs[5:]
    for i in range(7):
        loads[i].wait()
        at = slice(i * 512, (i + 1) * 512)
        zf[at] = zb[at].astype(F32) * scale
        if i < 6:
            to = (c2 if i < 3 else c1).at[(i % 3) * 512 : (i % 3 + 1) * 512]
            c = pltpu.make_async_copy(zf.at[at], to, os_.at[i])
        else:
            c = pltpu.make_async_copy(zf.at[3072:3552], proj, os_.at[i])
        c.start()
        moves.append(c)
        if 1 < i < 7:
            arrivals[i - 2].wait()
            c = pltpu.make_async_copy(held[i - 2], outs[i - 2], ds.at[i - 2])
            c.start()
            moves.append(c)
    vec[...] = zf[3552:3558]
    c = pltpu.make_async_copy(vec, vout, os_.at[7])
    c.start()
    for c in moves + [c]:
        c.wait()


ROW_SPLIT = P(None, ("table", "seq", "dp"))
HIST = ("table", "dp")
IN_SPECS = (ROW_SPLIT,) * 4 + (P(),) * 9 + (
    P(HIST, "seq", None, None), P(HIST, "seq", None), P(HIST, "seq", None, None), P(HIST, "seq", None, None),
    P(HIST, "seq", None),
)
OUT_SPECS = (P(HIST, "seq", None),) + (ROW_SPLIT,) * 4 + (P(),) * 4


def solution(mesh):
    return jax.shard_map(shards, mesh=mesh, in_specs=IN_SPECS, out_specs=OUT_SPECS, check_vma=False)
```

```python
import jax
import jax.numpy as jnp
from jax import lax
from jax.experimental import pallas as pl
from jax.experimental.pallas import tpu as pltpu
from jax.sharding import PartitionSpec as P

MESH = pl.DeviceIdType.MESH
F32, BF16, I32 = jnp.float32, jnp.bfloat16, jnp.int32
STEP = 4
EPS = 1e-5
NDEV, CAP, SLOTS, LEN, CH, ROWS = 128, 8, 1024, 512, 512, 2048
HALF = 256
BLK = 128
GC = 0.7978845608028654
GA = 0.044715
NT = (((1,), (1,)), ((), ()))
TN = (((0,), (0,)), ((), ()))
BASES = (0, 1536, 3072)
SPANS = (768, 768, 256)
AXES = ("x", "y", "z")


def dot(a, b, dims=None):
    if dims is None:
        return jnp.dot(a, b, preferred_element_type=F32)
    return lax.dot_general(a, b, dims, preferred_element_type=F32)


def gelu_parts(u):
    sq = u * u
    t = jnp.tanh(GC * (u + GA * u * sq))
    half = 0.5 * (1.0 + t)
    slope = half + (0.5 * GC) * u * (1.0 - t * t) * (1.0 + (3.0 * GA) * sq)
    return u * half, slope


def row_mean(v):
    return jnp.sum(v, axis=-1, keepdims=True) * (1.0 / CH)


def fold(v):
    return jnp.sum(v.reshape(v.shape[0] // 8, 8, v.shape[1]), axis=0)


def picked_lane(v, by_row):
    lane = lax.broadcasted_iota(I32, (NDEV, CAP, 128), 2)
    want = lax.broadcasted_iota(I32, (NDEV, CAP, 128), 1 if by_row else 0)
    if not by_row:
        want = want % 8
    one = jnp.sum(jnp.where(lane == want, v, 0.0), axis=-1, keepdims=True)
    return jnp.broadcast_to(one, (NDEV, CAP, 128)).reshape(SLOTS, 128)


def spread(v):
    return picked_lane(jnp.broadcast_to(v, (NDEV, CAP, 128)), 1)


def turned(v):
    full = jnp.concatenate([v, jnp.zeros((120, 128), F32)], axis=0)
    return full.T


def kernel(
    wide, mid, narrow, thin, proj, w1, w2, og,
    srow, sbandr, sevent, scount, b1, g1, o1, b2, g2, o2,
    block_out, t_wide, t_mid, t_narrow, t_thin, grads,
    tcat, pext, w1v, w2v, w1t, w2t, ogv, codes, relay, passed, fetched, code_sc, onehot, place, xin, msg, answers,
    eband, xm, e32, ehalo_s, ehalo_r, estack, hid, norm1, slope1, rstd1, a32, ahalo_s, ahalo_r, astack,
    bov, g2f, ghalo2_s, ghalo2_r, g1f, ghalo1_s, ghalo1_r, ge, gmsg, gotg, mt, tout,
    own_a, own_b, own_c, xs_a, xs_b, xs_c, xr_a, xr_b, xr_c, u_a, u_b, u_c,
    s1_r, s2_s, s2_r, s3_q, c1_r, c2_s, c2_r, c3_q, plane_r, zbuf,
    in_sem, rq_sem, ans_sem, halo_sem, gr_sem, core_sem, ar_sem, fin_sem, out_sem, loc_sem,
):
    t, s, d = lax.axis_index("table"), lax.axis_index("seq"), lax.axis_index("dp")
    sd = s * 4 + d
    me = t * 8 + sd
    coord = {"x": lax.rem(t, 4), "y": d, "z": t // 4}
    other = 1 - s

    def peer(axis, j):
        n = lax.rem(coord[axis] + j, 4)
        if axis == "x":
            return n, (t - coord["x"] + n, s, d)
        if axis == "y":
            return n, (t, s, n)
        return n, (n * 4 + coord["x"], s, d)

    def plane(b, c):
        for jb in range(4):
            for jc in range(4):
                if jb or jc:
                    n = {a: lax.rem(coord[a] + jb * (a == b) + jc * (a == c), 4) for a in AXES}
                    yield jb * 4 + jc - 1, n[b], n[c], (n["z"] * 4 + n["x"], s, n["y"])

    def dev(o):
        return (o // 8, lax.rem(o // 4, 2), lax.rem(o, 4))

    def rcopy(src, dst, send, recv, to):
        return pltpu.make_async_remote_copy(
            src_ref=src, dst_ref=dst, send_sem=send, recv_sem=recv, device_id=to, device_id_type=MESH
        )

    partner = (t, other, d)

    ins = [
        (wide, tcat.at[0:256]), (mid, tcat.at[256:384]), (narrow, tcat.at[384:448]),
        (thin, tcat.at[448:480]), (proj, pext.at[0:480]), (w1, w1v), (w2, w2v), (og, ogv),
    ]
    in_copies = [pltpu.make_async_copy(a, b, in_sem.at[i]) for i, (a, b) in enumerate(ins)]
    for c in in_copies:
        c.start()

    code_t = turned((srow[...] + ROWS * sbandr[...]).astype(F32)).reshape(16, 8, 128)
    asked = code_t[0]
    for k in range(1, 16):
        asked = asked + pltpu.roll(code_t[k], k * 8, 1)
    codes[...] = asked.astype(I32).reshape(8, 1, 128)

    pending = list(c.wait for c in in_copies)

    def finish():
        for f in pending:
            f()

    bar = pltpu.get_barrier_semaphore()

    def near(k):
        n = lax.rem(sd + k, 8)
        return n, (t, n // 4, lax.rem(n, 4))

    def far(k):
        n = lax.rem(t + k, 16)
        return n, (n, s, d)

    def sig_near(k, c):
        pl.semaphore_signal(bar, inc=1, device_id=near(k)[1], device_id_type=MESH)
        return c

    def sig_far(k, c):
        pl.semaphore_signal(bar, inc=1, device_id=far(k)[1], device_id_type=MESH)
        return c

    lax.fori_loop(1, 8, sig_near, 0)
    lax.fori_loop(1, 16, sig_far, 0)
    pl.semaphore_wait(bar, 22)

    def ask_near(k, c):
        n, to = near(k)
        rcopy(codes.at[n], relay.at[sd], rq_sem.at[0], rq_sem.at[1], to).start()
        return c

    lax.fori_loop(1, 8, ask_near, 0)
    relay[sd] = codes[sd]
    pext[480:512] = jnp.zeros((32, CH), BF16)
    tcat[480:512] = jnp.zeros((32, ROWS), BF16)

    w = rcopy(relay.at[pl.ds(0, 7)], relay.at[pl.ds(0, 7)], rq_sem.at[0], rq_sem.at[1], partner)
    w.wait_recv()
    pending.append(w.wait_send)

    passed[...] = turned(relay[...].reshape(8, 128).astype(F32)).astype(I32).reshape(16, 8, 128)

    def ask_far(k, c):
        n, to = far(k)
        rcopy(passed.at[n], fetched.at[t], rq_sem.at[2], rq_sem.at[3], to).start()
        return c

    lax.fori_loop(1, 16, ask_far, 0)
    fetched[t] = passed[t]
    w2nd = rcopy(fetched.at[pl.ds(0, 15)], fetched.at[pl.ds(0, 15)], rq_sem.at[2], rq_sem.at[3], partner)
    w2nd.wait_recv()
    pending.append(w2nd.wait_send)

    wide_f = jnp.broadcast_to(fetched[...].astype(F32).reshape(16, 1, 8, 128), (16, 8, 8, 128))
    code_sc[...] = picked_lane(wide_f.reshape(NDEV, CAP, 128), 0).astype(I32)

    for c in in_copies[:4]:
        c.wait()
    del pending[:4]

    lane128 = lax.broadcasted_iota(I32, (HALF, 128), 1)

    def lookup(i):
        cb = lax.rem(me // 32 + i, 4)
        rows = pl.ds(pl.multiple_of(cb * HALF, HALF), HALF)
        code = code_sc[rows]
        row, band = code & (ROWS - 1), code >> 11
        for b in range(ROWS // 128):
            onehot[rows, b * 128 : (b + 1) * 128] = (row == lane128 + b * 128).astype(F32).astype(BF16)
        got_rows = dot(onehot[rows], tcat[...], NT)
        first = jnp.where(
            band == 0, got_rows[:, 0:128], jnp.where(band == 1, got_rows[:, 256:384], got_rows[:, 384:512])
        )
        both = jnp.concatenate(
            [first.reshape(32, 8, 128), got_rows[:, 128:256].reshape(32, 8, 128)], axis=1
        )
        msg[pl.ds(cb * 32, 32)] = both.astype(BF16)

    def answer(i):
        cb = lax.rem(me // 32 + i, 4)
        for k in range(0 if i else 1, 32):
            to = cb * 32 + lax.rem(me + k, 32)
            rcopy(msg.at[to], answers.at[me], ans_sem.at[0], ans_sem.at[1], dev(to)).start()

    lookup(0)
    for i in range(4):
        answer(i)
        if i < 3:
            lookup(i + 1)

    live = lax.broadcasted_iota(I32, (CAP, NDEV), 0) < scount[...]
    target = spread(turned(jnp.where(live, sevent[...], LEN).astype(F32)).reshape(NDEV, 1, 128)).astype(I32)
    lane_p = lax.broadcasted_iota(I32, (SLOTS, 128), 1)
    for b in range(4):
        place[:, b * 128 : (b + 1) * 128] = (target == lane_p + b * 128).astype(F32).astype(BF16)
    xin[:, 256:384] = spread(turned(sbandr[...].astype(F32)).reshape(NDEV, 1, 128)).astype(BF16)
    answers[me] = msg[me]
    for c in in_copies[5:7]:
        c.wait()
    del pending[1:3]
    for k in range(3):
        at = slice(k * CH, (k + 1) * CH)
        w1t[at] = w1v[at].T
        w2t[at] = w2v[at].T
    wa = rcopy(msg.at[pl.ds(0, 127)], answers.at[pl.ds(0, 127)], ans_sem.at[0], ans_sem.at[1], partner)
    wa.wait_recv()
    pending.append(wa.wait_send)
    in_copies[4].wait()
    del pending[0]

    halves = answers[...].astype(F32)
    xin[:, 0:128] = halves[:, 0:8].reshape(SLOTS, 128).astype(BF16)
    xin[:, 128:256] = halves[:, 8:16].reshape(SLOTS, 128).astype(BF16)
    lane_e = lax.broadcasted_iota(I32, (LEN, 128), 1)
    x = dot(place[...], xin[...], TN)
    eb = x[:, 256:384]
    eband[...] = eb
    tail = ((eb == 2.0) & (lane_e < 64)) | ((eb == 3.0) & (lane_e >= 64) & (lane_e < 96))
    xm[:, 0:128] = jnp.where(eb == 0.0, x[:, 0:128], 0.0).astype(BF16)
    xm[:, 128:256] = jnp.where(eb == 0.0, x[:, 128:256], 0.0).astype(BF16)
    xm[:, 256:384] = jnp.where(eb == 1.0, x[:, 0:128], 0.0).astype(BF16)
    xm[:, 384:512] = jnp.where(tail, x[:, 0:128], 0.0).astype(BF16)

    def halo(i, src, dst):
        return rcopy(src, dst, halo_sem.at[2 * i], halo_sem.at[2 * i + 1], partner)

    hi, lo = slice(HALF, LEN), slice(0, HALF)
    e_hi = dot(xm[hi], pext[...]).astype(BF16)
    ehalo_s[...] = e_hi[HALF - 16 :]
    h_e = halo(0, ehalo_s, ehalo_r)
    h_e.start()
    e32[8 + HALF :] = e_hi.astype(F32)
    e_lo = dot(xm[lo], pext[...]).astype(BF16)
    e32[8 : 8 + HALF] = e_lo.astype(F32)

    def stack(part, src, dst, gap):
        base = 0 if part == "lo" else HALF
        for k in range(3):
            dst[base : base + HALF, k * CH : (k + 1) * CH] = src[
                base + (2 - k) * gap : base + (2 - k) * gap + HALF
            ].astype(BF16)

    first_core = s == 0

    def layer1(base):
        hid[...] = dot(estack[base : base + HALF], w1v[...]) + b1[...]

        def block(i, c):
            r0 = pl.multiple_of(i * BLK, BLK)
            h = hid[pl.ds(r0, BLK)]
            cen = h - row_mean(h)
            rs = lax.rsqrt(row_mean(cen * cen) + EPS)
            n = cen * rs
            act, slope = gelu_parts(n * g1[...] + o1[...])
            at = pl.ds(base + r0, BLK)
            norm1[at] = n
            slope1[at] = slope
            rstd1[at] = jnp.broadcast_to(rs, (BLK, 128))
            a32[pl.ds(base + r0 + 16, BLK)] = act.astype(BF16).astype(F32)
            return c

        lax.fori_loop(0, HALF // BLK, block, 0)

    pending.append(h_e.wait_send)
    stack("hi", e32, estack, STEP)
    layer1(HALF)
    ahalo_s[...] = a32[LEN:].astype(BF16)
    h_a = halo(1, ahalo_s, ahalo_r)
    h_a.start()
    h_e.wait_recv()
    e32[0:8] = jnp.where(first_core, 0.0, ehalo_r[...].astype(F32)[8:16])
    stack("lo", e32, estack, STEP)
    layer1(0)

    pending.append(h_a.wait_send)
    in_copies[7].wait()
    del pending[0]
    zero8 = jnp.zeros((8, CH), F32)

    def layer2(base, sums):
        hid[...] = dot(astack[base : base + HALF], w2v[...]) + b2[...]

        def block(i, c):
            r0 = pl.multiple_of(i * BLK, BLK)
            h = hid[pl.ds(r0, BLK)]
            cen = h - row_mean(h)
            rs = lax.rsqrt(row_mean(cen * cen) + EPS)
            n = cen * rs
            act, slope = gelu_parts(n * g2[...] + o2[...])
            at = pl.ds(base + r0, BLK)
            bov[at] = (e32[pl.ds(base + r0 + 8, BLK)] + act).astype(BF16)
            du = ogv[at].astype(F32) * slope
            dn = du * g2[...]
            dh = (rs * (dn - row_mean(dn) - n * row_mean(dn * n))).astype(BF16).astype(F32)
            g2f[at] = dh
            return (c[0] + fold(dh), c[1] + fold(du * n), c[2] + fold(du))

        return lax.fori_loop(0, HALF // BLK, block, sums)

    stack("hi", a32, astack, 2 * STEP)
    sums2 = layer2(HALF, (zero8, zero8, zero8))
    h_a.wait_recv()
    a32[0:16] = jnp.where(first_core, 0.0, ahalo_r[...].astype(F32))
    stack("lo", a32, astack, 2 * STEP)
    sums2 = layer2(0, sums2)
    ghalo2_s[...] = g2f[0:16].astype(BF16)
    h_g2 = halo(2, ghalo2_s, ghalo2_r)
    h_g2.start()
    out_bo = pltpu.make_async_copy(bov, block_out, out_sem.at[0])
    out_bo.start()
    pending += [h_g2.wait_send, out_bo.wait]

    owns, xss, xrs, us = (own_a, own_b, own_c), (xs_a, xs_b, xs_c), (xr_a, xr_b, xr_c), (u_a, u_b, u_c)

    def core_copy(g):
        return rcopy(xss[g], xrs[g], core_sem.at[2 * g], core_sem.at[2 * g + 1], partner)

    def parts_of(g):
        return (3 * g, 3 * g + 1, 3 * g + 2) if g < 2 else (6, 7)

    def first_row(p):
        return (p - 3 * min(p // 3, 2)) * (256 if p < 6 else 128)

    def order(p):
        k = (p + (p >= 6)) % 3
        return AXES[k], AXES[(k + 1) % 3], AXES[(k + 2) % 3]

    def sems(p, stage):
        return ar_sem.at[p * 10 + 2 * stage], ar_sem.at[p * 10 + 2 * stage + 1]

    def home(p):
        g = min(p // 3, 2)
        return pl.multiple_of(BASES[g] + s * SPANS[g] + first_row(p), 128)

    def chunk_rows(p):
        return 64 if p < 6 else 32

    def cut1(p, n):
        c = chunk_rows(p)
        return pl.ds(pl.multiple_of(first_row(p) + n * c, c), c)

    def cut2(ref, n):
        if ref.shape[0] == 64:
            return ref.at[pl.ds(pl.multiple_of(n * 16, 16), 16)]
        return ref.at[:, pl.ds(pl.multiple_of(n * 128, 128), 128)]

    def bufs(p):
        i = p if p < 6 else p - 6
        return tuple(r.at[i] for r in ((s1_r, s2_s, s2_r, s3_q) if p < 6 else (c1_r, c2_s, c2_r, c3_q)))

    def chunk_home(p, n):
        c = chunk_rows(p)
        return zbuf.at[pl.ds(pl.multiple_of(home(p) + n * c, c), c)]

    def last3(p, stage):
        if stage == 0:
            return bufs(p)[0]
        if stage == 1:
            return bufs(p)[2]
        if stage in (2, 3):
            return bufs(p)[3].at[pl.ds(0, 3)]
        return zbuf.at[pl.ds(0, 3 * chunk_rows(p))]

    def wait3(p, stage):
        send, recv = sems(p, stage)
        rcopy(last3(p, stage), last3(p, stage), send, recv, partner).wait_recv()
        pending.append(rcopy(last3(p, stage), last3(p, stage), send, recv, partner).wait_send)

    def tile(ref, i, j):
        return ref.at[pl.ds(pl.multiple_of(i * 16, 16), 16), pl.ds(pl.multiple_of(j * 128, 128), 128)]

    def wait15(p, stage):
        send, recv = sems(p, stage)
        ref = plane_r.at[p - 3]
        rcopy(ref, ref, send, recv, partner).wait_recv()
        pending.append(rcopy(ref, ref, send, recv, partner).wait_send)

    def plane_sum():
        for p in parts_of(1):
            a, b, c = order(p)
            wait15(p, 1)
            v = tile(s2_s.at[p], coord[b], coord[c])[...].astype(F32)
            for i in range(15):
                v = v + plane_r[p - 3, i].astype(F32)
            ref = tile(chunk_home(p, coord[a]), coord[b], coord[c])
            ref[...] = v.astype(BF16)
            send, recv = sems(p, 3)
            for _, _, _, to in plane(b, c):
                rcopy(ref, ref, send, recv, to).start()

    def ar_stage0(g):
        core_copy(g).wait_recv()
        pending.append(core_copy(g).wait_send)
        mine = owns[g][...] if g < 2 else own_c[pl.ds(pl.multiple_of(s * 256, 256), 256)]
        us[g][...] = (mine + xrs[g][...].astype(F32)).astype(BF16)
        for p in parts_of(g):
            send, recv = sems(p, 0)
            for j in (1, 2, 3):
                n, to = peer(order(p)[0], j)
                rcopy(us[g].at[cut1(p, n)], bufs(p)[0].at[j - 1], send, recv, to).start()

    def ar_stage1(g):
        for p in parts_of(g):
            a, b, _ = order(p)
            s1, s2s, s2r, _ = bufs(p)
            wait3(p, 0)
            v = us[g][cut1(p, coord[a])].astype(F32)
            for j in range(3):
                v = v + s1[j].astype(F32)
            s2s[...] = v.astype(BF16)
            send, recv = sems(p, 1)
            if g == 1:
                for i, nb, nc, to in plane(b, order(p)[2]):
                    rcopy(tile(s2s, nb, nc), plane_r.at[p - 3, i], send, recv, to).start()
                continue
            for j in (1, 2, 3):
                n, to = peer(b, j)
                rcopy(cut2(s2s, n), s2r.at[j - 1], send, recv, to).start()

    def ar_stage2(g):
        for p in parts_of(g):
            _, b, c = order(p)
            _, s2s, s2r, q = bufs(p)
            wait3(p, 1)
            v = cut2(s2s, coord[b])[...].astype(F32)
            for j in range(3):
                v = v + s2r[j].astype(F32)
            q[coord[c]] = v.astype(BF16)
            send, recv = sems(p, 2)
            for j in (1, 2, 3):
                _, to = peer(c, j)
                rcopy(q.at[coord[c]], q.at[coord[c]], send, recv, to).start()

    def ar_stage3(g):
        for p in parts_of(g):
            a, b, _ = order(p)
            wait3(p, 2)
            q = bufs(p)[3][...].astype(F32)
            to_ref = cut2(chunk_home(p, coord[a]), coord[b])
            to_ref[...] = (((q[0] + q[1]) + q[2]) + q[3]).astype(BF16)
            send, recv = sems(p, 3)
            for j in (1, 2, 3):
                _, to = peer(b, j)
                rcopy(to_ref, to_ref, send, recv, to).start()

    def ar_stage4(g):
        for p in parts_of(g):
            a = order(p)[0]
            (wait15 if g == 1 else wait3)(p, 3)
            ref = chunk_home(p, coord[a])
            send, recv = sems(p, 4)
            for j in (1, 2, 3):
                _, to = peer(a, j)
                rcopy(ref, ref, send, recv, to).start()

    def last_copy(p):
        ref = zbuf.at[pl.ds(home(p), 4 * chunk_rows(p))]
        return rcopy(ref, ref, fin_sem.at[2 * p], fin_sem.at[2 * p + 1], partner)

    def ar_stage5(g):
        for p in parts_of(g):
            wait3(p, 4)
            last_copy(p).start()
            write_out(p, s)

    def write_out(p, core):
        g = min(p // 3, 2)
        at = pl.ds(pl.multiple_of(BASES[g] + core * SPANS[g] + first_row(p), 128), 4 * chunk_rows(p))
        i = 5 + 2 * p
        sem = out_sem.at[i] if core is s else out_sem.at[i + 1]
        c = pltpu.make_async_copy(zbuf.at[at], grads.at[at], sem)
        c.start()
        pending.append(c.wait)

    def ar_finish(g):
        for p in parts_of(g):
            last_copy(p).wait()
            write_out(p, other)

    def weight_sum(g, taps, gb):
        theirs = pl.ds(pl.multiple_of(other * 768, 256), 768)
        mine = pl.ds(pl.multiple_of(s * 768, 256), 768)
        xss[g][...] = dot(taps[:, theirs], gb, TN).astype(BF16)
        core_copy(g).start()
        owns[g][...] = dot(taps[:, mine], gb, TN)

    weight_sum(0, astack, g2f[0:LEN].astype(BF16))

    def back1(base, sums):
        hid[...] = sum(
            dot(g2f[base + k * 8 : base + k * 8 + HALF].astype(BF16), w2t[k * CH : (k + 1) * CH])
            for k in range(3)
        )

        def block(i, c):
            r0 = pl.multiple_of(i * BLK, BLK)
            at = pl.ds(base + r0, BLK)
            n = norm1[at]
            du = hid[pl.ds(r0, BLK)] * slope1[at]
            dn = du * g1[...]
            rs = rstd1[at][:, 0:1]
            dh = (rs * (dn - row_mean(dn) - n * row_mean(dn * n))).astype(BF16).astype(F32)
            g1f[at] = dh
            return (c[0] + fold(dh), c[1] + fold(du * n), c[2] + fold(du))

        return lax.fori_loop(0, HALF // BLK, block, sums)

    sums1 = back1(0, (zero8, zero8, zero8))
    ghalo1_s[...] = g1f[0:16].astype(BF16)
    h_g1 = halo(3, ghalo1_s, ghalo1_r)
    h_g1.start()
    pending.append(h_g1.wait_send)
    ar_stage0(0)
    h_g2.wait_recv()
    g2f[LEN:] = jnp.where(first_core, ghalo2_r[...].astype(F32), 0.0)
    sums1 = back1(HALF, sums1)
    weight_sum(1, estack, g1f[0:LEN].astype(BF16))
    h_g1.wait_recv()
    g1f[LEN:] = jnp.where(first_core, ghalo1_r[...].astype(F32)[0:8], 0.0)

    def embed_grad(base):
        ge[base : base + HALF] = (
            ogv[base : base + HALF].astype(F32)
            + sum(
                dot(g1f[base + k * 4 : base + k * 4 + HALF].astype(BF16), w1t[k * CH : (k + 1) * CH])
                for k in range(3)
            )
        ).astype(BF16)

    embed_grad(0)
    ar_stage0(1)
    embed_grad(HALF)
    ar_stage1(0)

    own_c[...] = dot(xm[...], ge[...], TN)
    own_c[480:488] = jnp.concatenate(
        [jnp.sum(v, axis=0, keepdims=True) for v in (*sums1, *sums2)] + [jnp.zeros((2, CH), F32)], axis=0
    )
    xs_c[...] = own_c[pl.ds(pl.multiple_of(other * 256, 256), 256)].astype(BF16)
    core_copy(2).start()

    rg = dot(ge[...], pext[...], NT)
    first = jnp.where(eb == 0.0, rg[:, 0:128], jnp.where(eb == 1.0, rg[:, 256:384], rg[:, 384:512]))
    rgb = jnp.concatenate([first, rg[:, 128:256]], axis=1).astype(BF16)
    slots = dot(place[...], rgb)
    gmsg[...] = jnp.concatenate(
        [slots[:, 0:128].reshape(NDEV, 8, 128), slots[:, 128:256].reshape(NDEV, 8, 128)], axis=1
    ).astype(BF16)
    def send_grad(k, c):
        to = lax.rem(me + k, NDEV)
        rcopy(gmsg.at[to], gotg.at[me], gr_sem.at[0], gr_sem.at[1], dev(to)).start()
        return c

    gotg[me] = gmsg[me]

    def scatter():
        wg = rcopy(gmsg.at[pl.ds(0, 127)], gotg.at[pl.ds(0, 127)], gr_sem.at[0], gr_sem.at[1], partner)
        wg.wait_recv()
        pending.append(wg.wait_send)
        band = code_sc[...] >> 11
        lane_s = lax.broadcasted_iota(I32, (SLOTS, 128), 1)
        both = gotg[...].astype(F32)
        h0, h1 = both[:, 0:8].reshape(SLOTS, 128), both[:, 8:16].reshape(SLOTS, 128)
        tail = ((band == 2) & (lane_s < 64)) | ((band == 3) & (lane_s >= 64) & (lane_s < 96))
        mt[0:128] = jnp.where(band == 0, h0, 0.0).T.astype(BF16)
        mt[128:256] = jnp.where(band == 0, h1, 0.0).T.astype(BF16)
        mt[256:384] = jnp.where(band == 1, h0, 0.0).T.astype(BF16)
        mt[384:512] = jnp.where(tail, h0, 0.0).T.astype(BF16)
        for b in range(4):
            tout[:, b * 512 : (b + 1) * 512] = dot(mt[...], onehot[:, b * 512 : (b + 1) * 512]).astype(BF16)
        outs = [
            (tout.at[0:256], t_wide), (tout.at[256:384], t_mid),
            (tout.at[384:448], t_narrow), (tout.at[448:480], t_thin),
        ]
        for i, (a, b) in enumerate(outs):
            c = pltpu.make_async_copy(a, b, out_sem.at[1 + i])
            c.start()
            pending.append(c.wait)

    lax.fori_loop(1, NDEV, send_grad, 0)
    ar_stage2(0)
    ar_stage0(2)
    ar_stage1(1)
    ar_stage3(0)
    ar_stage1(2)
    plane_sum()
    ar_stage2(2)
    ar_stage4(0)
    ar_stage3(2)
    ar_stage4(1)
    scatter()
    ar_stage4(2)
    ar_stage5(0)
    ar_stage5(1)
    ar_stage5(2)
    ar_finish(0)
    ar_finish(1)
    ar_finish(2)
    finish()


def scratch():
    v = pltpu.VMEM
    dma = pltpu.SemaphoreType.DMA
    return [
        v((512, ROWS), BF16), v((512, CH), BF16), v((1536, CH), BF16), v((1536, CH), BF16), v((1536, CH), BF16), v((1536, CH), BF16), v((LEN, CH), BF16),
        v((8, 1, 128), I32), v((8, 1, 128), I32), v((16, 8, 128), I32), v((16, 8, 128), I32), v((SLOTS, 128), I32), v((SLOTS, ROWS), BF16),
        v((SLOTS, LEN), BF16), v((SLOTS, 384), BF16), v((NDEV, 16, 128), BF16), v((NDEV, 16, 128), BF16),
        v((LEN, 128), F32), v((LEN, 512), BF16), v((8 + LEN, CH), F32), v((16, CH), BF16), v((16, CH), BF16),
        v((LEN, 1536), BF16), v((HALF, CH), F32), v((LEN, CH), F32), v((LEN, CH), F32), v((LEN, 128), F32),
        v((16 + LEN, CH), F32), v((16, CH), BF16), v((16, CH), BF16), v((LEN, 1536), BF16),
        v((LEN, CH), BF16), v((LEN + 16, CH), F32), v((16, CH), BF16), v((16, CH), BF16),
        v((LEN + 8, CH), F32), v((16, CH), BF16), v((16, CH), BF16), v((LEN, CH), BF16),
        v((NDEV, 16, 128), BF16), v((NDEV, 16, 128), BF16), v((512, SLOTS), BF16), v((512, ROWS), BF16),
        v((768, CH), F32), v((768, CH), F32), v((512, CH), F32),
        v((768, CH), BF16), v((768, CH), BF16), v((256, CH), BF16),
        v((768, CH), BF16), v((768, CH), BF16), v((256, CH), BF16),
        v((768, CH), BF16), v((768, CH), BF16), v((256, CH), BF16),
        v((6, 3, 64, CH), BF16), v((6, 64, CH), BF16), v((6, 3, 16, CH), BF16), v((6, 4, 16, CH), BF16),
        v((2, 3, 32, CH), BF16), v((2, 32, CH), BF16), v((2, 3, 32, 128), BF16), v((2, 4, 32, 128), BF16),
        v((3, 15, 16, 128), BF16), v((3584, CH), BF16),
        dma((8,)), dma((4,)), dma((2,)), dma((8,)), dma((2,)), dma((6,)), dma((80,)), dma((16,)), dma((21,)), dma((1,)),
    ]


def shards(
    table_wide, table_mid, table_narrow, table_thin, band_proj, first_conv_weight, first_conv_bias,
    gain_first, offset_first, second_conv_weight, second_conv_bias, gain_second, offset_second,
    slot_event, slot_counts, slot_band, slot_row, out_grad,
):
    across = [v[0, 0].T for v in (slot_row, slot_band, slot_event)]
    vecs = [
        v.reshape(1, CH)
        for v in (first_conv_bias, gain_first, offset_first, second_conv_bias, gain_second, offset_second)
    ]
    hbm, vmem = pl.BlockSpec(memory_space=pl.ANY), pl.BlockSpec(memory_space=pltpu.VMEM)
    sds = jax.ShapeDtypeStruct
    block_out, tw, tm, tn, tt, grads = pl.pallas_call(
        kernel,
        out_shape=[
            sds((LEN, CH), BF16), sds((256, ROWS), BF16), sds((128, ROWS), BF16), sds((64, ROWS), BF16),
            sds((32, ROWS), BF16), sds((3584, CH), BF16),
        ],
        in_specs=[hbm] * 8 + [vmem] * 10,
        out_specs=[hbm] * 6,
        scratch_shapes=scratch(),
        compiler_params=pltpu.CompilerParams(
            collective_id=0, has_side_effects=True, vmem_limit_bytes=60 << 20
        ),
        cost_estimate=pl.CostEstimate(flops=12 * 10**9, bytes_accessed=14 * 2**20, transcendentals=2**19),
    )(
        table_wide, table_mid, table_narrow, table_thin, band_proj, first_conv_weight, second_conv_weight,
        out_grad[0], *across, slot_counts[0], *vecs,
    )
    copied = [block_out, tw, tm, tn, tt]
    outs = pl.pallas_call(
        finish_kernel,
        out_shape=[sds(v.shape, v.dtype) for v in copied]
        + [sds((480, CH), F32), sds((1536, CH), F32), sds((1536, CH), F32), sds((6, CH), F32)],
        in_specs=[hbm] * 6,
        out_specs=[hbm] * 9,
        scratch_shapes=[pltpu.VMEM(v.shape, v.dtype) for v in copied]
        + [
            pltpu.VMEM((3584, CH), BF16), pltpu.VMEM((3584, CH), F32), pltpu.VMEM((6, CH), F32),
            pltpu.SemaphoreType.DMA((5,)), pltpu.SemaphoreType.DMA((7,)), pltpu.SemaphoreType.DMA((8,)), pltpu.SemaphoreType.DMA((5,)),
        ],
        compiler_params=pltpu.CompilerParams(vmem_limit_bytes=60 << 20),
    )(*copied, grads)
    return (outs[0][None], *outs[1:])


def finish_kernel(*refs):
    copied, z, outs = refs[:5], refs[5], refs[6:15]
    held = refs[15:20]
    zb, zf, vec, cs, zs, os_, ds = refs[20:]
    loads = [
        pltpu.make_async_copy(z.at[i * 512 : (i + 1) * 512], zb.at[i * 512 : (i + 1) * 512], zs.at[i])
        for i in range(7)
    ]
    arrivals = [pltpu.make_async_copy(a, b, cs.at[i]) for i, (a, b) in enumerate(zip(copied, held))]
    for c in loads[:4] + arrivals + loads[4:]:
        c.start()
    moves = []
    scale = 1.0 / float(NDEV * LEN) ** 0.5
    proj, c1, c2, vout = outs[5:]
    for i in range(7):
        loads[i].wait()
        at = slice(i * 512, (i + 1) * 512)
        zf[at] = zb[at].astype(F32) * scale
        if i < 6:
            to = (c2 if i < 3 else c1).at[(i % 3) * 512 : (i % 3 + 1) * 512]
            c = pltpu.make_async_copy(zf.at[at], to, os_.at[i])
        else:
            c = pltpu.make_async_copy(zf.at[3072:3552], proj, os_.at[i])
        c.start()
        moves.append(c)
        if 1 < i < 7:
            arrivals[i - 2].wait()
            c = pltpu.make_async_copy(held[i - 2], outs[i - 2], ds.at[i - 2])
            c.start()
            moves.append(c)
    vec[...] = zf[3552:3558]
    c = pltpu.make_async_copy(vec, vout, os_.at[7])
    c.start()
    for c in moves + [c]:
        c.wait()


ROW_SPLIT = P(None, ("table", "seq", "dp"))
HIST = ("table", "dp")
IN_SPECS = (ROW_SPLIT,) * 4 + (P(),) * 9 + (
    P(HIST, "seq", None, None), P(HIST, "seq", None), P(HIST, "seq", None, None), P(HIST, "seq", None, None),
    P(HIST, "seq", None),
)
OUT_SPECS = (P(HIST, "seq", None),) + (ROW_SPLIT,) * 4 + (P(),) * 4


def solution(mesh):
    return jax.shard_map(shards, mesh=mesh, in_specs=IN_SPECS, out_specs=OUT_SPECS, check_vma=False)
```

```python
import jax
import jax.numpy as jnp
from jax import lax
from jax.experimental import pallas as pl
from jax.experimental.pallas import tpu as pltpu
from jax.sharding import PartitionSpec as P

MESH = pl.DeviceIdType.MESH
F32, BF16, I32 = jnp.float32, jnp.bfloat16, jnp.int32
STEP = 4
EPS = 1e-5
NDEV, CAP, SLOTS, LEN, CH, ROWS = 128, 8, 1024, 512, 512, 2048
HALF = 256
BLK = 128
GC = 0.7978845608028654
GA = 0.044715
NT = (((1,), (1,)), ((), ()))
TN = (((0,), (0,)), ((), ()))
BASES = (0, 1536, 3072)
SPANS = (768, 768, 256)
AXES = ("x", "y", "z")


def dot(a, b, dims=None):
    if dims is None:
        return jnp.dot(a, b, preferred_element_type=F32)
    return lax.dot_general(a, b, dims, preferred_element_type=F32)


def gelu_parts(u):
    sq = u * u
    t = jnp.tanh(GC * (u + GA * u * sq))
    half = 0.5 * (1.0 + t)
    slope = half + (0.5 * GC) * u * (1.0 - t * t) * (1.0 + (3.0 * GA) * sq)
    return u * half, slope


def row_mean(v):
    return jnp.sum(v, axis=-1, keepdims=True) * (1.0 / CH)


def fold(v):
    return jnp.sum(v.reshape(v.shape[0] // 8, 8, v.shape[1]), axis=0)


def picked_lane(v, by_row):
    lane = lax.broadcasted_iota(I32, (NDEV, CAP, 128), 2)
    want = lax.broadcasted_iota(I32, (NDEV, CAP, 128), 1 if by_row else 0)
    if not by_row:
        want = want % 8
    one = jnp.sum(jnp.where(lane == want, v, 0.0), axis=-1, keepdims=True)
    return jnp.broadcast_to(one, (NDEV, CAP, 128)).reshape(SLOTS, 128)


def spread(v):
    return picked_lane(jnp.broadcast_to(v, (NDEV, CAP, 128)), 1)


def turned(v):
    full = jnp.concatenate([v, jnp.zeros((120, 128), F32)], axis=0)
    return full.T


def kernel(
    wide, mid, narrow, thin, proj, w1, w2, og,
    srow, sbandr, sevent, scount, b1, g1, o1, b2, g2, o2,
    block_out, t_wide, t_mid, t_narrow, t_thin, grads,
    tcat, pext, w1v, w2v, w1t, w2t, ogv, codes, relay, passed, fetched, code_sc, onehot, place, xin, msg, answers,
    eband, xm, e32, ehalo_s, ehalo_r, estack, hid, norm1, slope1, rstd1, a32, ahalo_s, ahalo_r, astack,
    bov, g2f, ghalo2_s, ghalo2_r, g1f, ghalo1_s, ghalo1_r, ge, gmsg, gotg, mt, tout,
    own_a, own_b, own_c, xs_a, xs_b, xs_c, xr_a, xr_b, xr_c, u_a, u_b, u_c,
    s1_r, s2_s, s2_r, s3_q, c1_r, c2_s, c2_r, c3_q, plane_r, zbuf,
    in_sem, rq_sem, ans_sem, halo_sem, gr_sem, core_sem, ar_sem, fin_sem, out_sem, loc_sem,
):
    t, s, d = lax.axis_index("table"), lax.axis_index("seq"), lax.axis_index("dp")
    sd = s * 4 + d
    me = t * 8 + sd
    coord = {"x": lax.rem(t, 4), "y": d, "z": t // 4}
    other = 1 - s

    def peer(axis, j):
        n = lax.rem(coord[axis] + j, 4)
        if axis == "x":
            return n, (t - coord["x"] + n, s, d)
        if axis == "y":
            return n, (t, s, n)
        return n, (n * 4 + coord["x"], s, d)

    def plane(b, c):
        for jb in range(4):
            for jc in range(4):
                if jb or jc:
                    n = {a: lax.rem(coord[a] + jb * (a == b) + jc * (a == c), 4) for a in AXES}
                    yield jb * 4 + jc - 1, n[b], n[c], (n["z"] * 4 + n["x"], s, n["y"])

    def dev(o):
        return (o // 8, lax.rem(o // 4, 2), lax.rem(o, 4))

    def rcopy(src, dst, send, recv, to):
        return pltpu.make_async_remote_copy(
            src_ref=src, dst_ref=dst, send_sem=send, recv_sem=recv, device_id=to, device_id_type=MESH
        )

    partner = (t, other, d)

    ins = [
        (wide, tcat.at[0:256]), (mid, tcat.at[256:384]), (narrow, tcat.at[384:448]),
        (thin, tcat.at[448:480]), (proj, pext.at[0:480]), (w1, w1v), (w2, w2v), (og, ogv),
    ]
    in_copies = [pltpu.make_async_copy(a, b, in_sem.at[i]) for i, (a, b) in enumerate(ins)]
    for c in in_copies:
        c.start()

    code_t = turned((srow[...] + ROWS * sbandr[...]).astype(F32)).reshape(16, 8, 128)
    asked = code_t[0]
    for k in range(1, 16):
        asked = asked + pltpu.roll(code_t[k], k * 8, 1)
    codes[...] = asked.astype(I32).reshape(8, 1, 128)

    pending = list(c.wait for c in in_copies)

    def finish():
        for f in pending:
            f()

    bar = pltpu.get_barrier_semaphore()

    def near(k):
        n = lax.rem(sd + k, 8)
        return n, (t, n // 4, lax.rem(n, 4))

    def far(k):
        n = lax.rem(t + k, 16)
        return n, (n, s, d)

    def sig_near(k, c):
        pl.semaphore_signal(bar, inc=1, device_id=near(k)[1], device_id_type=MESH)
        return c

    def sig_far(k, c):
        pl.semaphore_signal(bar, inc=1, device_id=far(k)[1], device_id_type=MESH)
        return c

    lax.fori_loop(1, 8, sig_near, 0)
    lax.fori_loop(1, 16, sig_far, 0)
    pl.semaphore_wait(bar, 22)

    def ask_near(k, c):
        n, to = near(k)
        rcopy(codes.at[n], relay.at[sd], rq_sem.at[0], rq_sem.at[1], to).start()
        return c

    lax.fori_loop(1, 8, ask_near, 0)
    relay[sd] = codes[sd]
    pext[480:512] = jnp.zeros((32, CH), BF16)
    tcat[480:512] = jnp.zeros((32, ROWS), BF16)

    w = rcopy(relay.at[pl.ds(0, 7)], relay.at[pl.ds(0, 7)], rq_sem.at[0], rq_sem.at[1], partner)
    w.wait_recv()
    pending.append(w.wait_send)

    passed[...] = turned(relay[...].reshape(8, 128).astype(F32)).astype(I32).reshape(16, 8, 128)

    def ask_far(k, c):
        n, to = far(k)
        rcopy(passed.at[n], fetched.at[t], rq_sem.at[2], rq_sem.at[3], to).start()
        return c

    lax.fori_loop(1, 16, ask_far, 0)
    fetched[t] = passed[t]
    w2nd = rcopy(fetched.at[pl.ds(0, 15)], fetched.at[pl.ds(0, 15)], rq_sem.at[2], rq_sem.at[3], partner)
    w2nd.wait_recv()
    pending.append(w2nd.wait_send)

    wide_f = jnp.broadcast_to(fetched[...].astype(F32).reshape(16, 1, 8, 128), (16, 8, 8, 128))
    code_sc[...] = picked_lane(wide_f.reshape(NDEV, CAP, 128), 0).astype(I32)

    for c in in_copies[:4]:
        c.wait()
    del pending[:4]

    lane128 = lax.broadcasted_iota(I32, (HALF, 128), 1)

    def lookup(i):
        cb = lax.rem(me // 32 + i, 4)
        rows = pl.ds(pl.multiple_of(cb * HALF, HALF), HALF)
        code = code_sc[rows]
        row, band = code & (ROWS - 1), code >> 11
        for b in range(ROWS // 128):
            onehot[rows, b * 128 : (b + 1) * 128] = (row == lane128 + b * 128).astype(F32).astype(BF16)
        got_rows = dot(onehot[rows], tcat[...], NT)
        first = jnp.where(
            band == 0, got_rows[:, 0:128], jnp.where(band == 1, got_rows[:, 256:384], got_rows[:, 384:512])
        )
        both = jnp.concatenate(
            [first.reshape(32, 8, 128), got_rows[:, 128:256].reshape(32, 8, 128)], axis=1
        )
        msg[pl.ds(cb * 32, 32)] = both.astype(BF16)

    def answer(i):
        cb = lax.rem(me // 32 + i, 4)
        for k in range(0 if i else 1, 32):
            to = cb * 32 + lax.rem(me + k, 32)
            rcopy(msg.at[to], answers.at[me], ans_sem.at[0], ans_sem.at[1], dev(to)).start()

    lookup(0)
    for i in range(4):
        answer(i)
        if i < 3:
            lookup(i + 1)

    live = lax.broadcasted_iota(I32, (CAP, NDEV), 0) < scount[...]
    target = spread(turned(jnp.where(live, sevent[...], LEN).astype(F32)).reshape(NDEV, 1, 128)).astype(I32)
    lane_p = lax.broadcasted_iota(I32, (SLOTS, 128), 1)
    for b in range(4):
        place[:, b * 128 : (b + 1) * 128] = (target == lane_p + b * 128).astype(F32).astype(BF16)
    xin[:, 256:384] = spread(turned(sbandr[...].astype(F32)).reshape(NDEV, 1, 128)).astype(BF16)
    answers[me] = msg[me]
    for c in in_copies[5:7]:
        c.wait()
    del pending[1:3]
    for k in range(3):
        at = slice(k * CH, (k + 1) * CH)
        w1t[at] = w1v[at].T
        w2t[at] = w2v[at].T
    wa = rcopy(msg.at[pl.ds(0, 127)], answers.at[pl.ds(0, 127)], ans_sem.at[0], ans_sem.at[1], partner)
    wa.wait_recv()
    pending.append(wa.wait_send)
    in_copies[4].wait()
    del pending[0]

    halves = answers[...].astype(F32)
    xin[:, 0:128] = halves[:, 0:8].reshape(SLOTS, 128).astype(BF16)
    xin[:, 128:256] = halves[:, 8:16].reshape(SLOTS, 128).astype(BF16)
    lane_e = lax.broadcasted_iota(I32, (LEN, 128), 1)
    x = dot(place[...], xin[...], TN)
    eb = x[:, 256:384]
    eband[...] = eb
    tail = ((eb == 2.0) & (lane_e < 64)) | ((eb == 3.0) & (lane_e >= 64) & (lane_e < 96))
    xm[:, 0:128] = jnp.where(eb == 0.0, x[:, 0:128], 0.0).astype(BF16)
    xm[:, 128:256] = jnp.where(eb == 0.0, x[:, 128:256], 0.0).astype(BF16)
    xm[:, 256:384] = jnp.where(eb == 1.0, x[:, 0:128], 0.0).astype(BF16)
    xm[:, 384:512] = jnp.where(tail, x[:, 0:128], 0.0).astype(BF16)

    def halo(i, src, dst):
        return rcopy(src, dst, halo_sem.at[2 * i], halo_sem.at[2 * i + 1], partner)

    hi, lo = slice(HALF, LEN), slice(0, HALF)
    e_hi = dot(xm[hi], pext[...]).astype(BF16)
    ehalo_s[...] = e_hi[HALF - 16 :]
    h_e = halo(0, ehalo_s, ehalo_r)
    h_e.start()
    e32[8 + HALF :] = e_hi.astype(F32)
    e_lo = dot(xm[lo], pext[...]).astype(BF16)
    e32[8 : 8 + HALF] = e_lo.astype(F32)

    def stack(part, src, dst, gap):
        base = 0 if part == "lo" else HALF
        for k in range(3):
            dst[base : base + HALF, k * CH : (k + 1) * CH] = src[
                base + (2 - k) * gap : base + (2 - k) * gap + HALF
            ].astype(BF16)

    first_core = s == 0

    def layer1(base):
        hid[...] = dot(estack[base : base + HALF], w1v[...]) + b1[...]

        def block(i, c):
            r0 = pl.multiple_of(i * BLK, BLK)
            h = hid[pl.ds(r0, BLK)]
            cen = h - row_mean(h)
            rs = lax.rsqrt(row_mean(cen * cen) + EPS)
            n = cen * rs
            act, slope = gelu_parts(n * g1[...] + o1[...])
            at = pl.ds(base + r0, BLK)
            norm1[at] = n
            slope1[at] = slope
            rstd1[at] = jnp.broadcast_to(rs, (BLK, 128))
            a32[pl.ds(base + r0 + 16, BLK)] = act.astype(BF16).astype(F32)
            return c

        lax.fori_loop(0, HALF // BLK, block, 0)

    pending.append(h_e.wait_send)
    stack("hi", e32, estack, STEP)
    layer1(HALF)
    ahalo_s[...] = a32[LEN:].astype(BF16)
    h_a = halo(1, ahalo_s, ahalo_r)
    h_a.start()
    h_e.wait_recv()
    e32[0:8] = jnp.where(first_core, 0.0, ehalo_r[...].astype(F32)[8:16])
    stack("lo", e32, estack, STEP)
    layer1(0)

    pending.append(h_a.wait_send)
    in_copies[7].wait()
    del pending[0]
    zero8 = jnp.zeros((8, CH), F32)

    def layer2(base, sums):
        hid[...] = dot(astack[base : base + HALF], w2v[...]) + b2[...]

        def block(i, c):
            r0 = pl.multiple_of(i * BLK, BLK)
            h = hid[pl.ds(r0, BLK)]
            cen = h - row_mean(h)
            rs = lax.rsqrt(row_mean(cen * cen) + EPS)
            n = cen * rs
            act, slope = gelu_parts(n * g2[...] + o2[...])
            at = pl.ds(base + r0, BLK)
            bov[at] = (e32[pl.ds(base + r0 + 8, BLK)] + act).astype(BF16)
            du = ogv[at].astype(F32) * slope
            dn = du * g2[...]
            dh = (rs * (dn - row_mean(dn) - n * row_mean(dn * n))).astype(BF16).astype(F32)
            g2f[at] = dh
            return (c[0] + fold(dh), c[1] + fold(du * n), c[2] + fold(du))

        return lax.fori_loop(0, HALF // BLK, block, sums)

    stack("hi", a32, astack, 2 * STEP)
    sums2 = layer2(HALF, (zero8, zero8, zero8))
    h_a.wait_recv()
    a32[0:16] = jnp.where(first_core, 0.0, ahalo_r[...].astype(F32))
    stack("lo", a32, astack, 2 * STEP)
    sums2 = layer2(0, sums2)
    ghalo2_s[...] = g2f[0:16].astype(BF16)
    h_g2 = halo(2, ghalo2_s, ghalo2_r)
    h_g2.start()
    out_bo = pltpu.make_async_copy(bov, block_out, out_sem.at[0])
    out_bo.start()
    pending += [h_g2.wait_send, out_bo.wait]

    owns, xss, xrs, us = (own_a, own_b, own_c), (xs_a, xs_b, xs_c), (xr_a, xr_b, xr_c), (u_a, u_b, u_c)

    def core_copy(g):
        return rcopy(xss[g], xrs[g], core_sem.at[2 * g], core_sem.at[2 * g + 1], partner)

    def parts_of(g):
        return (3 * g, 3 * g + 1, 3 * g + 2) if g < 2 else (6, 7)

    def first_row(p):
        return (p - 3 * min(p // 3, 2)) * (256 if p < 6 else 128)

    def order(p):
        k = (p + (p >= 6)) % 3
        return AXES[k], AXES[(k + 1) % 3], AXES[(k + 2) % 3]

    def sems(p, stage):
        return ar_sem.at[p * 10 + 2 * stage], ar_sem.at[p * 10 + 2 * stage + 1]

    def home(p):
        g = min(p // 3, 2)
        return pl.multiple_of(BASES[g] + s * SPANS[g] + first_row(p), 128)

    def chunk_rows(p):
        return 64 if p < 6 else 32

    def cut1(p, n):
        c = chunk_rows(p)
        return pl.ds(pl.multiple_of(first_row(p) + n * c, c), c)

    def cut2(ref, n):
        if ref.shape[0] == 64:
            return ref.at[pl.ds(pl.multiple_of(n * 16, 16), 16)]
        return ref.at[:, pl.ds(pl.multiple_of(n * 128, 128), 128)]

    def bufs(p):
        i = p if p < 6 else p - 6
        return tuple(r.at[i] for r in ((s1_r, s2_s, s2_r, s3_q) if p < 6 else (c1_r, c2_s, c2_r, c3_q)))

    def chunk_home(p, n):
        c = chunk_rows(p)
        return zbuf.at[pl.ds(pl.multiple_of(home(p) + n * c, c), c)]

    def last3(p, stage):
        if stage == 0:
            return bufs(p)[0]
        if stage == 1:
            return bufs(p)[2]
        if stage in (2, 3):
            return bufs(p)[3].at[pl.ds(0, 3)]
        return zbuf.at[pl.ds(0, 3 * chunk_rows(p))]

    def wait3(p, stage):
        send, recv = sems(p, stage)
        rcopy(last3(p, stage), last3(p, stage), send, recv, partner).wait_recv()
        pending.append(rcopy(last3(p, stage), last3(p, stage), send, recv, partner).wait_send)

    def tile(ref, i, j):
        return ref.at[pl.ds(pl.multiple_of(i * 16, 16), 16), pl.ds(pl.multiple_of(j * 128, 128), 128)]

    def wait15(p, stage):
        send, recv = sems(p, stage)
        ref = plane_r.at[p - 3]
        rcopy(ref, ref, send, recv, partner).wait_recv()
        pending.append(rcopy(ref, ref, send, recv, partner).wait_send)

    def plane_sum():
        for p in parts_of(1):
            a, b, c = order(p)
            wait15(p, 1)
            v = tile(s2_s.at[p], coord[b], coord[c])[...].astype(F32)
            for i in range(15):
                v = v + plane_r[p - 3, i].astype(F32)
            ref = tile(chunk_home(p, coord[a]), coord[b], coord[c])
            ref[...] = v.astype(BF16)
            send, recv = sems(p, 3)
            for _, _, _, to in plane(b, c):
                rcopy(ref, ref, send, recv, to).start()

    def ar_stage0(g):
        core_copy(g).wait_recv()
        pending.append(core_copy(g).wait_send)
        mine = owns[g][...] if g < 2 else own_c[pl.ds(pl.multiple_of(s * 256, 256), 256)]
        us[g][...] = (mine + xrs[g][...].astype(F32)).astype(BF16)
        for p in parts_of(g):
            send, recv = sems(p, 0)
            for j in (1, 2, 3):
                n, to = peer(order(p)[0], j)
                rcopy(us[g].at[cut1(p, n)], bufs(p)[0].at[j - 1], send, recv, to).start()

    def ar_stage1(g):
        for p in parts_of(g):
            a, b, _ = order(p)
            s1, s2s, s2r, _ = bufs(p)
            wait3(p, 0)
            v = us[g][cut1(p, coord[a])].astype(F32)
            for j in range(3):
                v = v + s1[j].astype(F32)
            s2s[...] = v.astype(BF16)
            send, recv = sems(p, 1)
            if g == 1:
                for i, nb, nc, to in plane(b, order(p)[2]):
                    rcopy(tile(s2s, nb, nc), plane_r.at[p - 3, i], send, recv, to).start()
                continue
            for j in (1, 2, 3):
                n, to = peer(b, j)
                rcopy(cut2(s2s, n), s2r.at[j - 1], send, recv, to).start()

    def ar_stage2(g):
        for p in parts_of(g):
            _, b, c = order(p)
            _, s2s, s2r, q = bufs(p)
            wait3(p, 1)
            v = cut2(s2s, coord[b])[...].astype(F32)
            for j in range(3):
                v = v + s2r[j].astype(F32)
            q[coord[c]] = v.astype(BF16)
            send, recv = sems(p, 2)
            for j in (1, 2, 3):
                _, to = peer(c, j)
                rcopy(q.at[coord[c]], q.at[coord[c]], send, recv, to).start()

    def ar_stage3(g):
        for p in parts_of(g):
            a, b, _ = order(p)
            wait3(p, 2)
            q = bufs(p)[3][...].astype(F32)
            to_ref = cut2(chunk_home(p, coord[a]), coord[b])
            to_ref[...] = (((q[0] + q[1]) + q[2]) + q[3]).astype(BF16)
            send, recv = sems(p, 3)
            for j in (1, 2, 3):
                _, to = peer(b, j)
                rcopy(to_ref, to_ref, send, recv, to).start()

    def ar_stage4(g):
        for p in parts_of(g):
            a = order(p)[0]
            (wait15 if g == 1 else wait3)(p, 3)
            ref = chunk_home(p, coord[a])
            send, recv = sems(p, 4)
            for j in (1, 2, 3):
                _, to = peer(a, j)
                rcopy(ref, ref, send, recv, to).start()

    def last_copy(p):
        ref = zbuf.at[pl.ds(home(p), 4 * chunk_rows(p))]
        return rcopy(ref, ref, fin_sem.at[2 * p], fin_sem.at[2 * p + 1], partner)

    def ar_stage5(g):
        for p in parts_of(g):
            wait3(p, 4)
            last_copy(p).start()
            write_out(p, s)

    def write_out(p, core):
        g = min(p // 3, 2)
        at = pl.ds(pl.multiple_of(BASES[g] + core * SPANS[g] + first_row(p), 128), 4 * chunk_rows(p))
        i = 5 + 2 * p
        sem = out_sem.at[i] if core is s else out_sem.at[i + 1]
        c = pltpu.make_async_copy(zbuf.at[at], grads.at[at], sem)
        c.start()
        pending.append(c.wait)

    def ar_finish(g):
        for p in parts_of(g):
            last_copy(p).wait()
            write_out(p, other)

    def weight_sum(g, taps, gb):
        theirs = pl.ds(pl.multiple_of(other * 768, 256), 768)
        mine = pl.ds(pl.multiple_of(s * 768, 256), 768)
        xss[g][...] = dot(taps[:, theirs], gb, TN).astype(BF16)
        core_copy(g).start()
        owns[g][...] = dot(taps[:, mine], gb, TN)

    weight_sum(0, astack, g2f[0:LEN].astype(BF16))

    def back1(base, sums):
        hid[...] = sum(
            dot(g2f[base + k * 8 : base + k * 8 + HALF].astype(BF16), w2t[k * CH : (k + 1) * CH])
            for k in range(3)
        )

        def block(i, c):
            r0 = pl.multiple_of(i * BLK, BLK)
            at = pl.ds(base + r0, BLK)
            n = norm1[at]
            du = hid[pl.ds(r0, BLK)] * slope1[at]
            dn = du * g1[...]
            rs = rstd1[at][:, 0:1]
            dh = (rs * (dn - row_mean(dn) - n * row_mean(dn * n))).astype(BF16).astype(F32)
            g1f[at] = dh
            return (c[0] + fold(dh), c[1] + fold(du * n), c[2] + fold(du))

        return lax.fori_loop(0, HALF // BLK, block, sums)

    sums1 = back1(0, (zero8, zero8, zero8))
    ghalo1_s[...] = g1f[0:16].astype(BF16)
    h_g1 = halo(3, ghalo1_s, ghalo1_r)
    h_g1.start()
    pending.append(h_g1.wait_send)
    ar_stage0(0)
    h_g2.wait_recv()
    g2f[LEN:] = jnp.where(first_core, ghalo2_r[...].astype(F32), 0.0)
    sums1 = back1(HALF, sums1)
    weight_sum(1, estack, g1f[0:LEN].astype(BF16))
    h_g1.wait_recv()
    g1f[LEN:] = jnp.where(first_core, ghalo1_r[...].astype(F32)[0:8], 0.0)

    def embed_grad(base):
        ge[base : base + HALF] = (
            ogv[base : base + HALF].astype(F32)
            + sum(
                dot(g1f[base + k * 4 : base + k * 4 + HALF].astype(BF16), w1t[k * CH : (k + 1) * CH])
                for k in range(3)
            )
        ).astype(BF16)

    embed_grad(0)
    ar_stage0(1)
    embed_grad(HALF)
    ar_stage1(0)

    rg = dot(ge[...], pext[...], NT)
    first = jnp.where(eb == 0.0, rg[:, 0:128], jnp.where(eb == 1.0, rg[:, 256:384], rg[:, 384:512]))
    rgb = jnp.concatenate([first, rg[:, 128:256]], axis=1).astype(BF16)
    slots = dot(place[...], rgb)
    gmsg[...] = jnp.concatenate(
        [slots[:, 0:128].reshape(NDEV, 8, 128), slots[:, 128:256].reshape(NDEV, 8, 128)], axis=1
    ).astype(BF16)
    def send_grad(k, c):
        to = lax.rem(me + k, NDEV)
        rcopy(gmsg.at[to], gotg.at[me], gr_sem.at[0], gr_sem.at[1], dev(to)).start()
        return c

    gotg[me] = gmsg[me]

    def scatter():
        wg = rcopy(gmsg.at[pl.ds(0, 127)], gotg.at[pl.ds(0, 127)], gr_sem.at[0], gr_sem.at[1], partner)
        wg.wait_recv()
        pending.append(wg.wait_send)
        band = code_sc[...] >> 11
        lane_s = lax.broadcasted_iota(I32, (SLOTS, 128), 1)
        both = gotg[...].astype(F32)
        h0, h1 = both[:, 0:8].reshape(SLOTS, 128), both[:, 8:16].reshape(SLOTS, 128)
        tail = ((band == 2) & (lane_s < 64)) | ((band == 3) & (lane_s >= 64) & (lane_s < 96))
        mt[0:128] = jnp.where(band == 0, h0, 0.0).T.astype(BF16)
        mt[128:256] = jnp.where(band == 0, h1, 0.0).T.astype(BF16)
        mt[256:384] = jnp.where(band == 1, h0, 0.0).T.astype(BF16)
        mt[384:512] = jnp.where(tail, h0, 0.0).T.astype(BF16)
        for b in range(4):
            tout[:, b * 512 : (b + 1) * 512] = dot(mt[...], onehot[:, b * 512 : (b + 1) * 512]).astype(BF16)
        outs = [
            (tout.at[0:256], t_wide), (tout.at[256:384], t_mid),
            (tout.at[384:448], t_narrow), (tout.at[448:480], t_thin),
        ]
        for i, (a, b) in enumerate(outs):
            c = pltpu.make_async_copy(a, b, out_sem.at[1 + i])
            c.start()
            pending.append(c.wait)

    for k in range(1, NDEV):
        send_grad(k, 0)

    own_c[...] = dot(xm[...], ge[...], TN)
    own_c[480:488] = jnp.concatenate(
        [jnp.sum(v, axis=0, keepdims=True) for v in (*sums1, *sums2)] + [jnp.zeros((2, CH), F32)], axis=0
    )
    xs_c[...] = own_c[pl.ds(pl.multiple_of(other * 256, 256), 256)].astype(BF16)
    core_copy(2).start()

    ar_stage2(0)
    ar_stage0(2)
    ar_stage1(1)
    ar_stage3(0)
    ar_stage1(2)
    plane_sum()
    ar_stage2(2)
    ar_stage4(0)
    ar_stage3(2)
    ar_stage4(1)
    scatter()
    ar_stage4(2)
    ar_stage5(0)
    ar_stage5(1)
    ar_stage5(2)
    ar_finish(0)
    ar_finish(1)
    ar_finish(2)
    finish()


def scratch():
    v = pltpu.VMEM
    dma = pltpu.SemaphoreType.DMA
    return [
        v((512, ROWS), BF16), v((512, CH), BF16), v((1536, CH), BF16), v((1536, CH), BF16), v((1536, CH), BF16), v((1536, CH), BF16), v((LEN, CH), BF16),
        v((8, 1, 128), I32), v((8, 1, 128), I32), v((16, 8, 128), I32), v((16, 8, 128), I32), v((SLOTS, 128), I32), v((SLOTS, ROWS), BF16),
        v((SLOTS, LEN), BF16), v((SLOTS, 384), BF16), v((NDEV, 16, 128), BF16), v((NDEV, 16, 128), BF16),
        v((LEN, 128), F32), v((LEN, 512), BF16), v((8 + LEN, CH), F32), v((16, CH), BF16), v((16, CH), BF16),
        v((LEN, 1536), BF16), v((HALF, CH), F32), v((LEN, CH), F32), v((LEN, CH), F32), v((LEN, 128), F32),
        v((16 + LEN, CH), F32), v((16, CH), BF16), v((16, CH), BF16), v((LEN, 1536), BF16),
        v((LEN, CH), BF16), v((LEN + 16, CH), F32), v((16, CH), BF16), v((16, CH), BF16),
        v((LEN + 8, CH), F32), v((16, CH), BF16), v((16, CH), BF16), v((LEN, CH), BF16),
        v((NDEV, 16, 128), BF16), v((NDEV, 16, 128), BF16), v((512, SLOTS), BF16), v((512, ROWS), BF16),
        v((768, CH), F32), v((768, CH), F32), v((512, CH), F32),
        v((768, CH), BF16), v((768, CH), BF16), v((256, CH), BF16),
        v((768, CH), BF16), v((768, CH), BF16), v((256, CH), BF16),
        v((768, CH), BF16), v((768, CH), BF16), v((256, CH), BF16),
        v((6, 3, 64, CH), BF16), v((6, 64, CH), BF16), v((6, 3, 16, CH), BF16), v((6, 4, 16, CH), BF16),
        v((2, 3, 32, CH), BF16), v((2, 32, CH), BF16), v((2, 3, 32, 128), BF16), v((2, 4, 32, 128), BF16),
        v((3, 15, 16, 128), BF16), v((3584, CH), BF16),
        dma((8,)), dma((4,)), dma((2,)), dma((8,)), dma((2,)), dma((6,)), dma((80,)), dma((16,)), dma((21,)), dma((1,)),
    ]


def shards(
    table_wide, table_mid, table_narrow, table_thin, band_proj, first_conv_weight, first_conv_bias,
    gain_first, offset_first, second_conv_weight, second_conv_bias, gain_second, offset_second,
    slot_event, slot_counts, slot_band, slot_row, out_grad,
):
    across = [v[0, 0].T for v in (slot_row, slot_band, slot_event)]
    vecs = [
        v.reshape(1, CH)
        for v in (first_conv_bias, gain_first, offset_first, second_conv_bias, gain_second, offset_second)
    ]
    hbm, vmem = pl.BlockSpec(memory_space=pl.ANY), pl.BlockSpec(memory_space=pltpu.VMEM)
    sds = jax.ShapeDtypeStruct
    block_out, tw, tm, tn, tt, grads = pl.pallas_call(
        kernel,
        out_shape=[
            sds((LEN, CH), BF16), sds((256, ROWS), BF16), sds((128, ROWS), BF16), sds((64, ROWS), BF16),
            sds((32, ROWS), BF16), sds((3584, CH), BF16),
        ],
        in_specs=[hbm] * 8 + [vmem] * 10,
        out_specs=[hbm] * 6,
        scratch_shapes=scratch(),
        compiler_params=pltpu.CompilerParams(
            collective_id=0, has_side_effects=True, vmem_limit_bytes=60 << 20
        ),
        cost_estimate=pl.CostEstimate(flops=12 * 10**9, bytes_accessed=14 * 2**20, transcendentals=2**19),
    )(
        table_wide, table_mid, table_narrow, table_thin, band_proj, first_conv_weight, second_conv_weight,
        out_grad[0], *across, slot_counts[0], *vecs,
    )
    copied = [block_out, tw, tm, tn, tt]
    outs = pl.pallas_call(
        finish_kernel,
        out_shape=[sds(v.shape, v.dtype) for v in copied]
        + [sds((480, CH), F32), sds((1536, CH), F32), sds((1536, CH), F32), sds((6, CH), F32)],
        in_specs=[hbm] * 6,
        out_specs=[hbm] * 9,
        scratch_shapes=[pltpu.VMEM(v.shape, v.dtype) for v in copied]
        + [
            pltpu.VMEM((3584, CH), BF16), pltpu.VMEM((3584, CH), F32), pltpu.VMEM((6, CH), F32),
            pltpu.SemaphoreType.DMA((5,)), pltpu.SemaphoreType.DMA((7,)), pltpu.SemaphoreType.DMA((8,)), pltpu.SemaphoreType.DMA((5,)),
        ],
        compiler_params=pltpu.CompilerParams(vmem_limit_bytes=60 << 20),
    )(*copied, grads)
    return (outs[0][None], *outs[1:])


def finish_kernel(*refs):
    copied, z, outs = refs[:5], refs[5], refs[6:15]
    held = refs[15:20]
    zb, zf, vec, cs, zs, os_, ds = refs[20:]
    loads = [
        pltpu.make_async_copy(z.at[i * 512 : (i + 1) * 512], zb.at[i * 512 : (i + 1) * 512], zs.at[i])
        for i in range(7)
    ]
    arrivals = [pltpu.make_async_copy(a, b, cs.at[i]) for i, (a, b) in enumerate(zip(copied, held))]
    for c in loads[:4] + arrivals + loads[4:]:
        c.start()
    moves = []
    scale = 1.0 / float(NDEV * LEN) ** 0.5
    proj, c1, c2, vout = outs[5:]
    for i in range(7):
        loads[i].wait()
        at = slice(i * 512, (i + 1) * 512)
        zf[at] = zb[at].astype(F32) * scale
        if i < 6:
            to = (c2 if i < 3 else c1).at[(i % 3) * 512 : (i % 3 + 1) * 512]
            c = pltpu.make_async_copy(zf.at[at], to, os_.at[i])
        else:
            c = pltpu.make_async_copy(zf.at[3072:3552], proj, os_.at[i])
        c.start()
        moves.append(c)
        if 1 < i < 7:
            arrivals[i - 2].wait()
            c = pltpu.make_async_copy(held[i - 2], outs[i - 2], ds.at[i - 2])
            c.start()
            moves.append(c)
    vec[...] = zf[3552:3558]
    c = pltpu.make_async_copy(vec, vout, os_.at[7])
    c.start()
    for c in moves + [c]:
        c.wait()


ROW_SPLIT = P(None, ("table", "seq", "dp"))
HIST = ("table", "dp")
IN_SPECS = (ROW_SPLIT,) * 4 + (P(),) * 9 + (
    P(HIST, "seq", None, None), P(HIST, "seq", None), P(HIST, "seq", None, None), P(HIST, "seq", None, None),
    P(HIST, "seq", None),
)
OUT_SPECS = (P(HIST, "seq", None),) + (ROW_SPLIT,) * 4 + (P(),) * 4


def solution(mesh):
    return jax.shard_map(shards, mesh=mesh, in_specs=IN_SPECS, out_specs=OUT_SPECS, check_vma=False)
```
